32 devices in a mesh: group: 1, path: 32 (over z, y, x, core).
Axes of the slice: x: 2, y: 2, z: 4, core: 2. Of those that a mesh axis runs over, the one named last changes fastest.
Arguments:
- normals: float32 [8, 32, 8192], P(None, None, ('group', 'path')), may hold values from -6 to 6
- start_state: float32 [32, 8192], P(None, ('group', 'path')), may hold values from -0.12 to 0.12
- later_adjoint: float32 [32, 8192], P(None, ('group', 'path')), may hold values from -1.8 to 1.8
- vol: float32 [8], replicated, may hold values from 0.004 to 0.016
- factor_load: float32 [32, 960], replicated, may hold values from -2.1 to 2.1
- knots: float32 [960], replicated, may hold values from 0.01 to 0.05
- spline_jac: float32 [960, 960], replicated
- cashflows: bfloat16 [256, 960], P(('group', 'path')), may hold values from -0.1875 to 0.1875
- trade_set: int32 [256, 1], P(('group', 'path')), may hold values from 0 to 127
- trade_end: int32 [256], P(('group', 'path')), may hold values from 240 to 960
- set_cpty: int32 [128, 1], P('group'), may hold values from 0 to 63
- default_prob: float32 [8, 64], replicated, may hold values from 0.01 to 0.1
- base_value: float32 [8, 128], P(None, 'group'), may hold values from -3 to 3
Outputs:
- knot_grad: float32 [960], P('group')
- alloc: float32 [256], P(('group', 'path'))
- start_adjoint: float32 [32, 8192], P(None, ('group', 'path'))
The draws below stay inside these ranges and needn't reach their ends.
All inputs are finite; a program needn't handle non-finite values.
Results may differ from the reference program's by a relative error of at most 0.0011.
Values may be sent and summed in bfloat16 or wider, within the bound.
A program may use at most 64 MiB of HBM per device.

```python
import math
import jax
import jax.numpy as jnp
from jax import lax

K = 960
FACTORS = 32
DATES = 8
CPTY = 64
PATHS = 8192
TRADES = 256
NSETS = 128


def draw_spline_jac(key, part):
    first, second = jax.random.split(jax.random.fold_in(key, 11))
    diagonal = jax.random.uniform(first, (K,), jnp.float32, 0.6, 1.0)
    spread = jax.random.normal(second, (K, K), jnp.float32) * (0.3 / math.sqrt(K))
    return jnp.diag(diagonal) + spread


def draw_trade_end(key, part):
    shuffled = jax.random.permutation(jax.random.fold_in(key, 23), TRADES).astype(jnp.int32)
    return (K // 4 + shuffled * (K - K // 4) // (TRADES - 1)).astype(jnp.int32)


def shard_levels(stream_key, shape, cuts, low, high):
    gain = 1.0
    for dim, shards_of in cuts:
        steps = jax.random.uniform(jax.random.fold_in(jax.random.fold_in(stream_key, 6), dim), (shards_of,), jnp.float32, low / len(cuts), high / len(cuts))
        gain = gain * jnp.repeat(jnp.exp(steps), shape[dim] // shards_of).reshape((-1,) + (1,) * (len(shape) - 1 - dim))
    return gain


def picks_of(stream_key, rows, count, top, lift):
    ranking = jax.random.permutation(jax.random.fold_in(stream_key, 1), count)
    favour = ranking
    for power in range(3):
        favour = favour * favour // count
    favour = favour * lift // count
    lots = jax.random.randint(jax.random.fold_in(stream_key, 2), (rows, count), 0, 4096) + favour
    sure = jax.random.permutation(jax.random.fold_in(stream_key, 3), rows)[jnp.arange(count) % rows]
    lots = jnp.where(jnp.arange(rows)[:, None] == sure[None, :], 1 << 14, lots)
    score = lots * count + jnp.arange(count)
    return lax.top_k(score.astype(jnp.int32), top)[1].astype(jnp.int32)


def normal_values(key, extent, scale, bound, cuts=(), held_as=jnp.bfloat16):
    entries = scale * jax.random.normal(key, extent, jnp.float32)
    if cuts:
        entries = entries * shard_levels(key, extent, cuts, -0.22, 0.18)
    return jnp.clip(entries, -bound, bound).astype(held_as)


def setup_inputs(seed: int = 0, part: int = 0) -> dict:
    key_of = jax.random.split(jax.random.key(seed), 14)
    part_keys = jax.random.split(jax.random.fold_in(key_of[13], part), 14)
    normals = normal_values(part_keys[0], (DATES, FACTORS, PATHS), 1.0, 6.0, ((2, 32),), jnp.float32)
    start_state = normal_values(part_keys[1], (FACTORS, PATHS), 0.02, 0.12, ((1, 32),), jnp.float32)
    later_adjoint = normal_values(part_keys[2], (FACTORS, PATHS), 0.3, 1.8, ((1, 32),), jnp.float32)
    vol = jnp.clip(jnp.exp(jax.random.uniform(key_of[3], (DATES,), jnp.float32, math.log(0.004), math.log(0.016))), 0.004, 0.016)
    factor_load = normal_values(key_of[4], (FACTORS, K), 0.35, 2.1, (), jnp.float32)
    knots = jnp.clip(jax.random.uniform(key_of[5], (K,), jnp.float32, 0.01, 0.05), 0.01, 0.05)
    spline_jac = draw_spline_jac(jax.random.fold_in(key_of[13], 71), part)
    cashflows = normal_values(part_keys[7], (TRADES, K), K ** -0.5, 0.1875, ((0, 32),))
    trade_set = picks_of(part_keys[8], TRADES, NSETS, 1, 64)
    trade_end = draw_trade_end(jax.random.fold_in(jax.random.fold_in(key_of[13], part), 71), part)
    set_cpty = picks_of(part_keys[10], NSETS, CPTY, 1, 256)
    default_prob = jnp.clip(jnp.exp(jax.random.uniform(key_of[11], (DATES, CPTY), jnp.float32, math.log(0.01), math.log(0.1))), 0.01, 0.1)
    base_value = normal_values(part_keys[12], (DATES, NSETS), 0.5, 3.0, (), jnp.float32)
    return {"normals": normals, "start_state": start_state, "later_adjoint": later_adjoint, "vol": vol, "factor_load": factor_load, "knots": knots, "spline_jac": spline_jac, "cashflows": cashflows, "trade_set": trade_set, "trade_end": trade_end, "set_cpty": set_cpty, "default_prob": default_prob, "base_value": base_value}


MEAN_REV = 0.05
STEP_YEARS = 0.25
HORIZON_YEARS = 30.0
SHARPNESS = 4.0
LOSS_RATE = 0.6


def curve_terms(knots, spline_jac, date_count, knot_count):
    zero_rate = jnp.dot(spline_jac, knots, precision=lax.Precision.HIGHEST)
    knot_index = jnp.arange(knot_count, dtype=jnp.int32)
    date_index = jnp.arange(date_count, dtype=jnp.int32)
    is_alive = (120 * (knot_index[None, :] + 1)) > (knot_count * (date_index[:, None] + 1))
    maturity = HORIZON_YEARS * (knot_index + 1).astype(jnp.float32) / knot_count
    fixing = STEP_YEARS * (date_index + 1).astype(jnp.float32)
    horizon = jnp.where(is_alive, maturity[None, :] - fixing[:, None], jnp.float32(0.0))
    loading = (1.0 - jnp.exp(-MEAN_REV * horizon)) / MEAN_REV
    discount = jnp.where(is_alive, jnp.exp(-zero_rate[None, :] * horizon), jnp.float32(0.0))
    return horizon, loading, discount


def state_path(start_state, vol, normals):
    decay_factor = math.exp(-MEAN_REV * STEP_YEARS)
    state = start_state
    collected = []
    for index in range(normals.shape[0]):
        state = decay_factor * state + vol[index] * normals[index]
        collected.append(state)
    return jnp.stack(collected)


def reference(normals, start_state, later_adjoint, vol, factor_load, knots, spline_jac, cashflows, trade_set, trade_end, set_cpty, default_prob, base_value):
    highest = lax.Precision.HIGHEST
    horizon, loading, discount = curve_terms(knots, spline_jac, DATES, K)
    knot_index = jnp.arange(K, dtype=jnp.int32)
    live_flows = jnp.where(knot_index[None, :] < trade_end[:, None], cashflows, jnp.zeros_like(cashflows))
    set_ids = trade_set[:, 0]
    net_flows = jax.ops.segment_sum(live_flows.astype(jnp.float32), set_ids, num_segments=NSETS).astype(jnp.bfloat16)
    net_wide = net_flows.astype(jnp.float32)
    weight = LOSS_RATE * default_prob[:, set_cpty[:, 0]]
    block_size = math.gcd(PATHS, 2048)
    block_count = PATHS // block_size
    states = state_path(start_state, vol, normals)
    blocked = states.reshape(DATES, FACTORS, block_count, block_size).transpose(2, 0, 1, 3)

    def block_values(block_states):
        shift = jnp.einsum('fm,ifp->imp', factor_load, block_states, precision=highest)
        bond_term = jnp.exp(-loading[:, :, None] * shift)
        feat_exact = discount[:, :, None] * bond_term
        features = feat_exact.astype(jnp.bfloat16)
        values = jnp.einsum('nm,imp->inp', net_wide, features.astype(jnp.float32), precision=highest)
        return bond_term, feat_exact, features, values

    def sum_values(running, block_states):
        return running + jnp.sum(block_values(block_states)[3], axis=2), None

    running, _ = lax.scan(sum_values, jnp.zeros((DATES, NSETS), jnp.float32), blocked)
    mean_value = running / PATHS

    def slopes(values):
        shifted = values - mean_value[:, :, None] + base_value[:, :, None]
        return weight[:, :, None] * jax.nn.sigmoid(SHARPNESS * shifted)

    def sum_slopes(running, block_states):
        return running + jnp.sum(slopes(block_values(block_states)[3]), axis=2), None

    slope_total, _ = lax.scan(sum_slopes, jnp.zeros((DATES, NSETS), jnp.float32), blocked)
    mean_slope = slope_total / PATHS

    def backward(carry, block_states):
        discount_grad, load_sums = carry
        bond_term, feat_exact, features, values = block_values(block_states)
        set_adjoint = (slopes(values) - mean_slope[:, :, None]).astype(jnp.bfloat16)
        feat_adjoint = jnp.einsum('nm,inp->imp', net_wide, set_adjoint.astype(jnp.float32), precision=highest)
        state_local = -jnp.einsum('fm,imp->ifp', factor_load, feat_adjoint * feat_exact * loading[:, :, None], precision=highest)
        discount_grad = discount_grad + jnp.sum(feat_adjoint * bond_term, axis=2)
        load_sums = load_sums + jnp.einsum('inp,imp->nm', set_adjoint.astype(jnp.float32), features.astype(jnp.float32), precision=highest)
        return (discount_grad, load_sums), state_local

    init = (jnp.zeros((DATES, K), jnp.float32), jnp.zeros((NSETS, K), jnp.float32))
    (discount_grad, load_sums), local_blocks = lax.scan(backward, init, blocked)
    state_local = local_blocks.transpose(1, 2, 0, 3).reshape(DATES, FACTORS, PATHS)
    rate_adjoint = -jnp.sum(discount_grad * discount * horizon, axis=0) / PATHS
    knot_grad = jnp.dot(spline_jac.T, rate_adjoint, precision=highest)
    load_sums = load_sums / PATHS
    alloc = jnp.sum(live_flows.astype(jnp.float32) * load_sums[set_ids], axis=1)
    decay_factor = math.exp(-MEAN_REV * STEP_YEARS)
    carried = later_adjoint + state_local[DATES - 1]
    for index in reversed(range(DATES - 1)):
        carried = state_local[index] + decay_factor * carried
    start_adjoint = decay_factor * carried
    return knot_grad, alloc, start_adjoint
```

```python
import functools
import math

import jax
import jax.numpy as jnp
from jax import lax
from jax.experimental import pallas as pl
from jax.experimental.pallas import tpu as pltpu
from jax.sharding import PartitionSpec as P

MEAN_REV = 0.05
STEP_YEARS = 0.25
HORIZON_YEARS = 30.0
SHARPNESS = 4.0
LOSS_RATE = 0.6
DECAY = math.exp(-MEAN_REV * STEP_YEARS)
MESH = pl.DeviceIdType.MESH
F32 = jnp.float32
BF16 = jnp.bfloat16


def dot(a, b, dims, precision=None):
    return lax.dot_general(
        a, b, (dims, ((), ())), preferred_element_type=F32, precision=precision
    )


NN = ((1,), (0,))
NT = ((1,), (1,))
TN = ((0,), (0,))


def split3(x):
    high = x.astype(BF16)
    rest = x - high.astype(F32)
    mid = rest.astype(BF16)
    low = (rest - mid.astype(F32)).astype(BF16)
    return high, mid, low


def split2(x):
    high = x.astype(BF16)
    return high, (x - high.astype(F32)).astype(BF16)


def diagonal(rows):
    return lax.broadcasted_iota(jnp.int32, (rows, rows), 0) == lax.broadcasted_iota(
        jnp.int32, (rows, rows), 1
    )


def column_to_row(column):
    count = column.shape[0]
    pieces = []
    for first in range(0, count, 128):
        rows = min(128, count - first)
        piece = jnp.broadcast_to(column[first : first + rows], (rows, rows))
        pieces.append(jnp.sum(jnp.where(diagonal(rows), piece, 0.0), axis=0, keepdims=True))
    return jnp.concatenate(pieces, axis=1) if len(pieces) > 1 else pieces[0]


def row_to_column(row):
    count = row.shape[1]
    pieces = []
    for first in range(0, count, 128):
        rows = min(128, count - first)
        piece = jnp.broadcast_to(row[:, first : first + rows], (rows, rows))
        pieces.append(jnp.sum(jnp.where(diagonal(rows), piece, 0.0), axis=1, keepdims=True))
    return jnp.concatenate(pieces, axis=0) if len(pieces) > 1 else pieces[0]


def kernel(
    n,
    vol,
    trade_end,
    normals,
    start_state,
    later_adjoint,
    factor_load,
    knots,
    spline_hbm,
    cashflows,
    trade_set,
    set_cpty,
    default_prob,
    base_value,
    knot_out,
    alloc_out,
    start_out,
    spline,
    flows,
    value_sums,
    slope_sums,
    rate_sums,
    alloc_sent,
    alloc_sums,
    net,
    exact,
    features,
    values,
    adjoint,
    weighted,
    rate_acc,
    loading_rows,
    discount_rows,
    horizon_rows,
    weight_rows,
    load_split,
    spline_sem,
    send_sems,
    recv_sems,
):
    dates, factors, paths = normals.shape
    grid = knots.shape[1]
    trades = cashflows.shape[0]
    sets = base_value.shape[1]
    half = flows.shape[3] - sets
    chips = n // 2
    paths_all = paths * n
    me = lax.axis_index("path")
    chip, core = me // 2, me % 2
    partner = me + 1 - 2 * core

    spline_copy = pltpu.make_async_copy(spline_hbm, spline, spline_sem)
    spline_copy.start()

    barrier = pltpu.get_barrier_semaphore()

    def greet(step, carry):
        pl.semaphore_signal(
            barrier, inc=1, device_id={"path": lax.rem(me + step, n)}, device_id_type=MESH
        )
        return carry

    lax.fori_loop(1, n, greet, 0)

    end = jnp.zeros((trades, 1), jnp.int32)
    for trade in range(trades):
        at = lax.broadcasted_iota(jnp.int32, (trades, 1), 0) == trade
        end = jnp.where(at, trade_end[trade], end)
    live = jnp.where(
        lax.broadcasted_iota(jnp.int32, (trades, grid), 1) < end,
        cashflows[...].astype(F32),
        0.0,
    )
    upper = jnp.concatenate(
        [live[:, half:], jnp.zeros((trades, 2 * half - grid), F32)], axis=1
    )
    one_hot = (lax.broadcasted_iota(jnp.int32, (trades, sets), 1) == trade_set[...]).astype(F32)
    message = jnp.concatenate(
        [
            jnp.concatenate([live[:, :half], upper], axis=0),
            jnp.concatenate([one_hot, one_hot], axis=0),
        ],
        axis=1,
    )
    flows[core, chip] = message.astype(BF16)

    pl.semaphore_wait(barrier, n - 1)

    def send_flows(step, carry):
        pltpu.make_async_remote_copy(
            src_ref=flows.at[core, chip],
            dst_ref=flows.at[core, chip],
            send_sem=send_sems.at[0],
            recv_sem=recv_sems.at[0],
            device_id={"path": lax.rem(me + 2 * step, n)},
            device_id_type=MESH,
        ).start()
        return carry

    lax.fori_loop(1, chips, send_flows, 0)

    def send_all(buffer, which):
        def send(step, carry):
            pltpu.make_async_remote_copy(
                src_ref=buffer.at[me],
                dst_ref=buffer.at[me],
                send_sem=send_sems.at[which],
                recv_sem=recv_sems.at[which],
                device_id={"path": lax.rem(me + step, n)},
                device_id_type=MESH,
            ).start()
            return carry

        lax.fori_loop(1, n, send, 0)

    def wait_all(buffer, sems, which):
        others = buffer.at[pl.ds(0, n - 1)]
        pltpu.make_async_copy(others, others, sems.at[which]).wait()

    index = lax.broadcasted_iota(jnp.int32, (dates, grid), 1)
    date = lax.broadcasted_iota(jnp.int32, (dates, grid), 0)
    alive = 120 * (index + 1) > grid * (date + 1)
    maturity = HORIZON_YEARS * (index + 1).astype(F32) / grid
    fixing = STEP_YEARS * (date + 1).astype(F32)
    horizon = jnp.where(alive, maturity - fixing, 0.0)
    horizon_rows[...] = horizon
    loading_rows[...] = (1.0 - jnp.exp(-MEAN_REV * horizon)) / MEAN_REV
    spline_copy.wait()
    zero_rate = column_to_row(jnp.sum(spline[...] * knots[...], axis=1, keepdims=True))
    discount_rows[...] = jnp.where(alive, jnp.exp(-zero_rate * horizon), 0.0)

    counter = (
        lax.broadcasted_iota(jnp.int32, (sets, default_prob.shape[1]), 1) == set_cpty[...]
    ).astype(F32)
    weight_rows[...] = LOSS_RATE * dot(
        default_prob[...], counter, NT, precision=lax.Precision.HIGHEST
    )

    high, mid, low = split3(factor_load[...])
    load_split[...] = jnp.concatenate([high, high, mid, high, mid, low], axis=0)

    def forward(i, state):
        state = DECAY * state + vol[i] * normals[i]
        s_high, s_mid, s_low = split3(state)
        stacked = jnp.concatenate([s_high, s_mid, s_high, s_low, s_mid, s_high], axis=0)
        shift = dot(stacked, load_split[...], TN)
        bond = jnp.exp(-(loading_rows[pl.ds(i, 1), :] * shift))
        feat = discount_rows[pl.ds(i, 1), :] * bond
        exact[i] = feat
        features[i] = feat.astype(BF16)
        return state

    early = dates - dates // 4
    state = lax.fori_loop(0, early, forward, start_state[...])
    part = flows.at[0, pl.ds(0, chips - 1)]
    pltpu.make_async_copy(part, part, recv_sems.at[0]).wait()
    share = pltpu.make_async_remote_copy(
        src_ref=flows.at[core],
        dst_ref=flows.at[core],
        send_sem=send_sems.at[1],
        recv_sem=recv_sems.at[1],
        device_id={"path": partner},
        device_id_type=MESH,
    )
    share.start()
    lax.fori_loop(early, dates, forward, state)
    pltpu.make_async_copy(part, part, send_sems.at[0]).wait()
    share.wait()

    rows = n * 2 * trades
    all_flows = flows[:, :, :, :half].reshape(rows, half)
    member = flows[:, :, :, half:].reshape(rows, sets)
    is_upper = (lax.broadcasted_iota(jnp.int32, (rows, sets), 0) // trades) % 2 == 1
    member_wide = member.astype(F32)
    member_low = jnp.where(is_upper, 0.0, member_wide).astype(BF16)
    member_high = jnp.where(is_upper, member_wide, 0.0).astype(BF16)
    net[:, :half] = dot(member_low, all_flows, TN).astype(BF16)
    net[:, half:] = dot(member_high, all_flows, TN)[:, : grid - half].astype(BF16)

    def value(i, carry):
        found = dot(features[i], net[...], NT)
        values[i] = found
        value_sums[me, pl.ds(i, 1), :] = jnp.sum(found, axis=0, keepdims=True)
        return carry

    lax.fori_loop(0, dates, value, 0)
    send_all(value_sums, 2)
    wait_all(value_sums, recv_sems, 2)
    offset = base_value[...] - jnp.sum(value_sums[...], axis=0) / paths_all
    weights = weight_rows[...]
    for i in range(dates):
        shifted = values[i] + offset[i : i + 1]
        slope = weights[i : i + 1] * jax.nn.sigmoid(SHARPNESS * shifted)
        values[i] = slope
        slope_sums[me, i : i + 1, :] = jnp.sum(slope, axis=0, keepdims=True)
    send_all(slope_sums, 3)
    weighted[...] = jnp.zeros_like(weighted)
    rate_acc[...] = jnp.zeros_like(rate_acc)
    wait_all(slope_sums, recv_sems, 3)
    loading_rows[...] = loading_rows[...] * jnp.exp(
        lax.broadcasted_iota(jnp.int32, (dates, grid), 0).astype(F32)
        * (-MEAN_REV * STEP_YEARS)
    )
    weight_rows[...] = jnp.sum(slope_sums[...], axis=0) / paths_all

    def backward(i, carry):
        adj = (values[i] - weight_rows[pl.ds(i, 1), :]).astype(BF16)
        adjoint[pl.ds(pl.multiple_of(i * paths, paths), paths), :] = adj
        product = dot(adj, net[...], NN) * exact[i]
        weighted[...] += loading_rows[pl.ds(i, 1), :] * product
        folded = jnp.sum(product.reshape(paths // 8, 8, grid), axis=0)
        rate_acc[...] += horizon_rows[pl.ds(i, 1), :] * folded
        return carry

    lax.fori_loop(0, dates, backward, 0)
    rate = jnp.sum(rate_acc[...], axis=0, keepdims=True) * (-1.0 / paths_all)
    lines = rate_sums.shape[1]
    for line in range(lines):
        first = 128 * line
        if first < grid:
            piece = rate[:, first : first + 128]
            rate_sums[me, line : line + 1, : piece.shape[1]] = piece
            if piece.shape[1] < 128:
                rate_sums[me, line : line + 1, piece.shape[1] :] = jnp.zeros(
                    (1, 128 - piece.shape[1]), F32
                )
        else:
            rate_sums[me, line : line + 1, :] = jnp.zeros((1, 128), F32)
    send_all(rate_sums, 4)

    sums = dot(adjoint[...], features[...].reshape(dates * paths, grid), TN) * (1.0 / paths_all)
    sums = jnp.concatenate([sums, jnp.zeros((sets, 2 * half - grid), F32)], axis=1)
    stacked = jnp.concatenate(split2(sums), axis=0)
    low_part = dot(all_flows, stacked[:, :half], NT)
    high_part = dot(all_flows, stacked[:, half:], NT)
    low_part = low_part[:, :sets] + low_part[:, sets:]
    high_part = high_part[:, :sets] + high_part[:, sets:]
    terms = jnp.where(is_upper, high_part, low_part) * member_wide
    terms = terms.reshape(2, chips, 2, trades, sets)
    alloc_sent[...] = terms[:, :, 0] + terms[:, :, 1]
    alloc_sums[me] = alloc_sent[core, chip]

    def send_alloc(step, carry):
        other = lax.rem(me + step, n)
        pltpu.make_async_remote_copy(
            src_ref=alloc_sent.at[other % 2, other // 2],
            dst_ref=alloc_sums.at[me],
            send_sem=send_sems.at[5],
            recv_sem=recv_sems.at[5],
            device_id={"path": other},
            device_id_type=MESH,
        ).start()
        return carry

    lax.fori_loop(1, n, send_alloc, 0)

    load_high, load_low = split2(factor_load[...])
    y_high, y_low = split2(weighted[...])
    local = dot(jnp.concatenate([load_high, load_low], axis=0), y_high, NT)
    local = local[:factors] + local[factors:] + dot(load_high, y_low, NT)
    start_out[...] = DECAY**dates * later_adjoint[...] - DECAY * local

    wait_all(rate_sums, recv_sems, 4)
    total = jnp.sum(rate_sums[...], axis=0)
    column = row_to_column(
        jnp.concatenate([total[line : line + 1] for line in range(lines)], axis=1)[:, :grid]
    )
    knot_out[...] = jnp.sum(spline[...] * column, axis=0, keepdims=True)

    wait_all(alloc_sums, recv_sems, 5)
    alloc_out[...] = column_to_row(
        jnp.sum(jnp.sum(alloc_sums[...], axis=0), axis=1, keepdims=True)
    )
    for buffer, which in ((value_sums, 2), (slope_sums, 3), (rate_sums, 4), (alloc_sums, 5)):
        wait_all(buffer, send_sems, which)


def per_device(
    normals,
    start_state,
    later_adjoint,
    vol,
    factor_load,
    knots,
    spline_jac,
    cashflows,
    trade_set,
    trade_end,
    set_cpty,
    default_prob,
    base_value,
):
    n = lax.axis_size("path")
    dates, factors, paths = normals.shape
    grid = knots.shape[0]
    trades = cashflows.shape[0]
    sets = base_value.shape[1]
    half = -(-grid // 256) * 128
    lines = -(-grid // 1024) * 8
    vmem = pl.BlockSpec(memory_space=pltpu.VMEM)
    smem = pl.BlockSpec(memory_space=pltpu.SMEM)
    knot_grad, alloc, start_adjoint = pl.pallas_call(
        functools.partial(kernel, n),
        out_shape=[
            jax.ShapeDtypeStruct((1, grid), F32),
            jax.ShapeDtypeStruct((1, trades), F32),
            jax.ShapeDtypeStruct((factors, paths), F32),
        ],
        in_specs=[smem, smem] + [vmem] * 5 + [pl.BlockSpec(memory_space=pl.ANY)] + [vmem] * 5,
        out_specs=[vmem] * 3,
        scratch_shapes=[
            pltpu.VMEM((grid, grid), F32),
            pltpu.VMEM((2, n // 2, 2 * trades, half + sets), BF16),
            pltpu.VMEM((n, dates, sets), F32),
            pltpu.VMEM((n, dates, sets), F32),
            pltpu.VMEM((n, lines, 128), F32),
            pltpu.VMEM((2, n // 2, trades, sets), F32),
            pltpu.VMEM((n, trades, sets), F32),
            pltpu.VMEM((sets, grid), BF16),
            pltpu.VMEM((dates, paths, grid), F32),
            pltpu.VMEM((dates, paths, grid), BF16),
            pltpu.VMEM((dates, paths, sets), F32),
            pltpu.VMEM((dates * paths, sets), BF16),
            pltpu.VMEM((paths, grid), F32),
            pltpu.VMEM((8, grid), F32),
            pltpu.VMEM((dates, grid), F32),
            pltpu.VMEM((dates, grid), F32),
            pltpu.VMEM((dates, grid), F32),
            pltpu.VMEM((dates, sets), F32),
            pltpu.VMEM((6 * factors, grid), BF16),
            pltpu.SemaphoreType.DMA,
            pltpu.SemaphoreType.DMA((6,)),
            pltpu.SemaphoreType.DMA((6,)),
        ],
        compiler_params=pltpu.CompilerParams(
            collective_id=0, has_side_effects=True, vmem_limit_bytes=56 * 1024 * 1024
        ),
    )(
        vol,
        trade_end,
        normals,
        start_state,
        later_adjoint,
        factor_load,
        knots.reshape(1, grid),
        spline_jac,
        cashflows,
        trade_set,
        set_cpty,
        default_prob,
        base_value,
    )
    return knot_grad.reshape(grid), alloc.reshape(trades), start_adjoint


def solution(mesh):
    in_specs = (
        P(None, None, ("group", "path")),
        P(None, ("group", "path")),
        P(None, ("group", "path")),
        P(),
        P(),
        P(),
        P(),
        P(("group", "path"), None),
        P(("group", "path"), None),
        P(("group", "path")),
        P("group", None),
        P(),
        P(None, "group"),
    )
    out_specs = (P("group"), P(("group", "path")), P(None, ("group", "path")))
    return jax.shard_map(
        per_device, mesh=mesh, in_specs=in_specs, out_specs=out_specs, check_vma=False
    )
```

```python
import functools
import math

import jax
import jax.numpy as jnp
from jax import lax
from jax.experimental import pallas as pl
from jax.experimental.pallas import tpu as pltpu
from jax.sharding import PartitionSpec as P

MEAN_REV = 0.05
STEP_YEARS = 0.25
HORIZON_YEARS = 30.0
SHARPNESS = 4.0
LOSS_RATE = 0.6
DECAY = math.exp(-MEAN_REV * STEP_YEARS)
MESH = pl.DeviceIdType.MESH
F32 = jnp.float32
BF16 = jnp.bfloat16


def dot(a, b, dims, precision=None):
    return lax.dot_general(
        a, b, (dims, ((), ())), preferred_element_type=F32, precision=precision
    )


NN = ((1,), (0,))
NT = ((1,), (1,))
TN = ((0,), (0,))


def split3(x):
    high = x.astype(BF16)
    rest = x - high.astype(F32)
    mid = rest.astype(BF16)
    low = (rest - mid.astype(F32)).astype(BF16)
    return high, mid, low


def split2(x):
    high = x.astype(BF16)
    return high, (x - high.astype(F32)).astype(BF16)


def diagonal(rows):
    return lax.broadcasted_iota(jnp.int32, (rows, rows), 0) == lax.broadcasted_iota(
        jnp.int32, (rows, rows), 1
    )


def column_to_row(column):
    count = column.shape[0]
    pieces = []
    for first in range(0, count, 128):
        rows = min(128, count - first)
        piece = jnp.broadcast_to(column[first : first + rows], (rows, rows))
        pieces.append(jnp.sum(jnp.where(diagonal(rows), piece, 0.0), axis=0, keepdims=True))
    return jnp.concatenate(pieces, axis=1) if len(pieces) > 1 else pieces[0]


def row_to_column(row):
    count = row.shape[1]
    pieces = []
    for first in range(0, count, 128):
        rows = min(128, count - first)
        piece = jnp.broadcast_to(row[:, first : first + rows], (rows, rows))
        pieces.append(jnp.sum(jnp.where(diagonal(rows), piece, 0.0), axis=1, keepdims=True))
    return jnp.concatenate(pieces, axis=0) if len(pieces) > 1 else pieces[0]


def kernel(
    n,
    vol,
    trade_set,
    trade_end,
    normals,
    start_state,
    factor_load,
    knots,
    spline_hbm,
    cashflows,
    set_cpty,
    default_prob,
    base_value,
    knot_out,
    alloc_out,
    start_out,
    spline,
    flows,
    value_pair,
    value_sums,
    slope_pair,
    slope_sums,
    rate_pair,
    rate_sums,
    alloc_sent,
    alloc_pair,
    alloc_chip,
    alloc_sums,
    net,
    exact,
    features,
    values,
    adjoint,
    weighted,
    rate_acc,
    loading_rows,
    discount_rows,
    horizon_rows,
    weight_rows,
    load_split,
    spline_sem,
    send_sems,
    recv_sems,
):
    dates, factors, paths = normals.shape
    grid = knots.shape[1]
    trades = cashflows.shape[0]
    sets = base_value.shape[1]
    half = flows.shape[3] - sets
    chips = n // 2
    paths_all = paths * n
    me = lax.axis_index("path")
    chip, core = me // 2, me % 2
    partner = me + 1 - 2 * core

    spline_copy = pltpu.make_async_copy(spline_hbm, spline, spline_sem)
    spline_copy.start()

    barrier = pltpu.get_barrier_semaphore()

    def greet(step, carry):
        pl.semaphore_signal(
            barrier, inc=1, device_id={"path": lax.rem(me + 2 * step, n)}, device_id_type=MESH
        )
        return carry

    lax.fori_loop(1, chips, greet, 0)
    pl.semaphore_signal(barrier, inc=1, device_id={"path": partner}, device_id_type=MESH)

    end = jnp.zeros((trades, 1), jnp.int32)
    set_id = jnp.zeros((trades, 1), jnp.int32)
    for trade in range(trades):
        at = lax.broadcasted_iota(jnp.int32, (trades, 1), 0) == trade
        end = jnp.where(at, trade_end[trade], end)
        set_id = jnp.where(at, trade_set[trade], set_id)
    live = jnp.where(
        lax.broadcasted_iota(jnp.int32, (trades, grid), 1) < end,
        cashflows[...].astype(F32),
        0.0,
    )
    upper = jnp.concatenate(
        [live[:, half:], jnp.zeros((trades, 2 * half - grid), F32)], axis=1
    )
    one_hot = (lax.broadcasted_iota(jnp.int32, (trades, sets), 1) == set_id).astype(F32)
    message = jnp.concatenate(
        [
            jnp.concatenate([live[:, :half], upper], axis=0),
            jnp.concatenate([one_hot, one_hot], axis=0),
        ],
        axis=1,
    )
    flows[core, chip] = message.astype(BF16)

    pl.semaphore_wait(barrier, chips)

    def send_flows(step, carry):
        pltpu.make_async_remote_copy(
            src_ref=flows.at[core, chip],
            dst_ref=flows.at[core, chip],
            send_sem=send_sems.at[0],
            recv_sem=recv_sems.at[0],
            device_id={"path": lax.rem(me + 2 * step, n)},
            device_id_type=MESH,
        ).start()
        return carry

    lax.fori_loop(1, chips, send_flows, 0)

    def send_pair(buffer, target, which):
        copy = pltpu.make_async_remote_copy(
            src_ref=buffer,
            dst_ref=target,
            send_sem=send_sems.at[which],
            recv_sem=recv_sems.at[which],
            device_id={"path": partner},
            device_id_type=MESH,
        )
        copy.start()
        return copy

    def send_chips(source, buffer, which):
        def send(step, carry):
            other = lax.rem(chip + step, chips)
            pltpu.make_async_remote_copy(
                src_ref=source(other),
                dst_ref=buffer.at[chip],
                send_sem=send_sems.at[which],
                recv_sem=recv_sems.at[which],
                device_id={"path": 2 * other + core},
                device_id_type=MESH,
            ).start()
            return carry

        lax.fori_loop(1, chips, send, 0)

    def wait_chips(buffer, sems, which):
        others = buffer.at[pl.ds(0, chips - 1)]
        pltpu.make_async_copy(others, others, sems.at[which]).wait()

    def send_sum(pair, sums, which):
        sums[chip] = pair[0] + pair[1]
        send_chips(lambda other: sums.at[chip], sums, which)

    index = lax.broadcasted_iota(jnp.int32, (dates, grid), 1)
    date = lax.broadcasted_iota(jnp.int32, (dates, grid), 0)
    alive = 120 * (index + 1) > grid * (date + 1)
    maturity = HORIZON_YEARS * (index + 1).astype(F32) / grid
    fixing = STEP_YEARS * (date + 1).astype(F32)
    horizon = jnp.where(alive, maturity - fixing, 0.0)
    horizon_rows[...] = horizon
    loading_rows[...] = (1.0 - jnp.exp(-MEAN_REV * horizon)) / MEAN_REV
    spline_copy.wait()
    zero_rate = column_to_row(jnp.sum(spline[...] * knots[...], axis=1, keepdims=True))
    discount_rows[...] = jnp.where(alive, jnp.exp(-zero_rate * horizon), 0.0)

    counter = (
        lax.broadcasted_iota(jnp.int32, (default_prob.shape[1], sets), 0) == set_cpty[...]
    ).astype(F32)
    weight_rows[...] = LOSS_RATE * dot(
        default_prob[...], counter, NN, precision=lax.Precision.HIGHEST
    )

    high, mid, low = split3(factor_load[...])
    load_split[...] = jnp.concatenate([high, high, mid, high, mid, low], axis=0)

    def forward(i, state):
        state = DECAY * state + vol[i] * normals[i]
        s_high, s_mid, s_low = split3(state)
        stacked = jnp.concatenate([s_high, s_mid, s_high, s_low, s_mid, s_high], axis=0)
        shift = dot(stacked, load_split[...], TN)
        bond = jnp.exp(-(loading_rows[pl.ds(i, 1), :] * shift))
        feat = discount_rows[pl.ds(i, 1), :] * bond
        exact[i] = feat
        features[i] = feat.astype(BF16)
        return state

    early = dates - dates // 4
    state = lax.fori_loop(0, early, forward, start_state[...])
    part = flows.at[0, pl.ds(0, chips - 1)]
    pltpu.make_async_copy(part, part, recv_sems.at[0]).wait()
    share = pltpu.make_async_remote_copy(
        src_ref=flows.at[core],
        dst_ref=flows.at[core],
        send_sem=send_sems.at[1],
        recv_sem=recv_sems.at[1],
        device_id={"path": partner},
        device_id_type=MESH,
    )
    share.start()
    lax.fori_loop(early, dates, forward, state)
    pltpu.make_async_copy(part, part, send_sems.at[0]).wait()
    share.wait()

    rows = n * 2 * trades
    all_flows = flows[:, :, :, :half].reshape(rows, half)
    member = flows[:, :, :, half:].reshape(rows, sets)
    is_upper = (lax.broadcasted_iota(jnp.int32, (rows, sets), 0) // trades) % 2 == 1
    member_wide = member.astype(F32)
    member_low = jnp.where(is_upper, 0.0, member_wide).astype(BF16)
    member_high = jnp.where(is_upper, member_wide, 0.0).astype(BF16)
    net[:, :half] = dot(member_low, all_flows, TN).astype(BF16)
    net[:, half:] = dot(member_high, all_flows, TN)[:, : grid - half].astype(BF16)

    def value(i, carry):
        found = dot(features[i], net[...], NT)
        values[i] = found
        value_pair[core, pl.ds(i, 1), :] = jnp.sum(found, axis=0, keepdims=True)
        return carry

    lax.fori_loop(0, dates, value, 0)
    send_pair(value_pair.at[core], value_pair.at[core], 2).wait()
    send_sum(value_pair, value_sums, 3)
    wait_chips(value_sums, recv_sems, 3)
    offset = base_value[...] - jnp.sum(value_sums[...], axis=0) / paths_all
    weights = weight_rows[...]
    for i in range(dates):
        shifted = values[i] + offset[i : i + 1]
        slope = weights[i : i + 1] * jax.nn.sigmoid(SHARPNESS * shifted)
        values[i] = slope
        slope_pair[core, i : i + 1, :] = jnp.sum(slope, axis=0, keepdims=True)
    send_pair(slope_pair.at[core], slope_pair.at[core], 4).wait()
    send_sum(slope_pair, slope_sums, 5)
    weighted[...] = jnp.zeros_like(weighted)
    rate_acc[...] = jnp.zeros_like(rate_acc)
    wait_chips(slope_sums, recv_sems, 5)
    loading_rows[...] = loading_rows[...] * jnp.exp(
        lax.broadcasted_iota(jnp.int32, (dates, grid), 0).astype(F32)
        * (-MEAN_REV * STEP_YEARS)
    )
    weight_rows[...] = jnp.sum(slope_sums[...], axis=0) / paths_all

    def backward(i, carry):
        adj = (values[i] - weight_rows[pl.ds(i, 1), :]).astype(BF16)
        adjoint[pl.ds(pl.multiple_of(i * paths, paths), paths), :] = adj
        product = dot(adj, net[...], NN) * exact[i]
        weighted[...] += loading_rows[pl.ds(i, 1), :] * product
        folded = jnp.sum(product.reshape(paths // 8, 8, grid), axis=0)
        rate_acc[...] += horizon_rows[pl.ds(i, 1), :] * folded
        return carry

    lax.fori_loop(0, dates, backward, 0)
    rate = jnp.sum(rate_acc[...], axis=0, keepdims=True) * (-1.0 / paths_all)
    lines = rate_sums.shape[1]
    for line in range(lines):
        first = 128 * line
        if first < grid:
            piece = rate[:, first : first + 128]
            rate_pair[core, line : line + 1, : piece.shape[1]] = piece
            if piece.shape[1] < 128:
                rate_pair[core, line : line + 1, piece.shape[1] :] = jnp.zeros(
                    (1, 128 - piece.shape[1]), F32
                )
        else:
            rate_pair[core, line : line + 1, :] = jnp.zeros((1, 128), F32)
    rate_copy = send_pair(rate_pair.at[core], rate_pair.at[core], 6)

    sums = dot(adjoint[...], features[...].reshape(dates * paths, grid), TN) * (1.0 / paths_all)
    sums = jnp.concatenate([sums, jnp.zeros((sets, 2 * half - grid), F32)], axis=1)
    stacked = jnp.concatenate(split2(sums), axis=0)
    low_part = dot(all_flows, stacked[:, :half], NT)
    high_part = dot(all_flows, stacked[:, half:], NT)
    low_part = low_part[:, :sets] + low_part[:, sets:]
    high_part = high_part[:, :sets] + high_part[:, sets:]
    terms = jnp.where(is_upper, high_part, low_part) * member_wide
    terms = terms.reshape(2, chips, 2, trades, sets)
    alloc_sent[...] = terms[:, :, 0] + terms[:, :, 1]
    alloc_copy = send_pair(alloc_sent.at[1 - core], alloc_pair, 8)
    rate_copy.wait()
    send_sum(rate_pair, rate_sums, 7)

    load_high, load_low = split2(factor_load[...])
    y_high, y_low = split2(weighted[...])
    local = dot(jnp.concatenate([load_high, load_low], axis=0), y_high, NT)
    local = local[:factors] + local[factors:] + dot(load_high, y_low, NT)
    start_out[...] = local
    alloc_copy.wait()
    alloc_chip[...] = alloc_sent[core] + alloc_pair[...]
    alloc_sums[chip] = alloc_chip[chip]
    send_chips(lambda other: alloc_chip.at[other], alloc_sums, 9)

    wait_chips(rate_sums, recv_sems, 7)
    total = jnp.sum(rate_sums[...], axis=0)
    column = row_to_column(
        jnp.concatenate([total[line : line + 1] for line in range(lines)], axis=1)[:, :grid]
    )
    knot_out[...] = jnp.sum(spline[...] * column, axis=0, keepdims=True)

    wait_chips(alloc_sums, recv_sems, 9)
    alloc_out[...] = column_to_row(
        jnp.sum(jnp.sum(alloc_sums[...], axis=0), axis=1, keepdims=True)
    )
    for buffer, which in ((value_sums, 3), (slope_sums, 5), (rate_sums, 7), (alloc_sums, 9)):
        wait_chips(buffer, send_sems, which)


def finish(knot_part, alloc_part, local, later_adjoint, knot_out, alloc_out, start_out, *, dates):
    knot_out[...] = knot_part[...]
    alloc_out[...] = alloc_part[...]
    start_out[...] = DECAY**dates * later_adjoint[...] - DECAY * local[...]


def per_device(
    normals,
    start_state,
    later_adjoint,
    vol,
    factor_load,
    knots,
    spline_jac,
    cashflows,
    trade_set,
    trade_end,
    set_cpty,
    default_prob,
    base_value,
):
    n = lax.axis_size("path")
    dates, factors, paths = normals.shape
    grid = knots.shape[0]
    trades = cashflows.shape[0]
    sets = base_value.shape[1]
    half = -(-grid // 256) * 128
    lines = -(-grid // 1024) * 8
    vmem = pl.BlockSpec(memory_space=pltpu.VMEM)
    smem = pl.BlockSpec(memory_space=pltpu.SMEM)
    out_shape = [
        jax.ShapeDtypeStruct((1, grid), F32),
        jax.ShapeDtypeStruct((1, trades), F32),
        jax.ShapeDtypeStruct((factors, paths), F32),
    ]
    parts = pl.pallas_call(
        functools.partial(kernel, n),
        out_shape=out_shape,
        in_specs=[smem] * 3 + [vmem] * 4 + [pl.BlockSpec(memory_space=pltpu.HBM)] + [vmem] * 4,
        out_specs=[vmem] * 3,
        scratch_shapes=[
            pltpu.VMEM((grid, grid), F32),
            pltpu.VMEM((2, n // 2, 2 * trades, half + sets), BF16),
            pltpu.VMEM((2, dates, sets), F32),
            pltpu.VMEM((n // 2, dates, sets), F32),
            pltpu.VMEM((2, dates, sets), F32),
            pltpu.VMEM((n // 2, dates, sets), F32),
            pltpu.VMEM((2, lines, 128), F32),
            pltpu.VMEM((n // 2, lines, 128), F32),
            pltpu.VMEM((2, n // 2, trades, sets), F32),
            pltpu.VMEM((n // 2, trades, sets), F32),
            pltpu.VMEM((n // 2, trades, sets), F32),
            pltpu.VMEM((n // 2, trades, sets), F32),
            pltpu.VMEM((sets, grid), BF16),
            pltpu.VMEM((dates, paths, grid), F32),
            pltpu.VMEM((dates, paths, grid), BF16),
            pltpu.VMEM((dates, paths, sets), F32),
            pltpu.VMEM((dates * paths, sets), BF16),
            pltpu.VMEM((paths, grid), F32),
            pltpu.VMEM((8, grid), F32),
            pltpu.VMEM((dates, grid), F32),
            pltpu.VMEM((dates, grid), F32),
            pltpu.VMEM((dates, grid), F32),
            pltpu.VMEM((dates, sets), F32),
            pltpu.VMEM((6 * factors, grid), BF16),
            pltpu.SemaphoreType.DMA,
            pltpu.SemaphoreType.DMA((10,)),
            pltpu.SemaphoreType.DMA((10,)),
        ],
        compiler_params=pltpu.CompilerParams(
            collective_id=0, has_side_effects=True, vmem_limit_bytes=50 * 1024 * 1024
        ),
    )(
        vol,
        trade_set.reshape(trades),
        trade_end,
        normals,
        start_state,
        factor_load,
        knots.reshape(1, grid),
        spline_jac,
        cashflows,
        set_cpty.reshape(1, sets),
        default_prob,
        base_value,
    )
    knot_grad, alloc, start_adjoint = pl.pallas_call(
        functools.partial(finish, dates=dates),
        out_shape=out_shape,
        in_specs=[vmem] * 4,
        out_specs=[vmem] * 3,
    )(*parts, later_adjoint)
    return knot_grad.reshape(grid), alloc.reshape(trades), start_adjoint


def solution(mesh):
    in_specs = (
        P(None, None, ("group", "path")),
        P(None, ("group", "path")),
        P(None, ("group", "path")),
        P(),
        P(),
        P(),
        P(),
        P(("group", "path"), None),
        P(("group", "path"), None),
        P(("group", "path")),
        P("group", None),
        P(),
        P(None, "group"),
    )
    out_specs = (P("group"), P(("group", "path")), P(None, ("group", "path")))
    return jax.shard_map(
        per_device, mesh=mesh, in_specs=in_specs, out_specs=out_specs, check_vma=False
    )
```

```python
import functools
import math

import jax
import jax.numpy as jnp
from jax import lax
from jax.experimental import pallas as pl
from jax.experimental.pallas import tpu as pltpu
from jax.sharding import PartitionSpec as P

MEAN_REV = 0.05
STEP_YEARS = 0.25
HORIZON_YEARS = 30.0
SHARPNESS = 4.0
LOSS_RATE = 0.6
DECAY = math.exp(-MEAN_REV * STEP_YEARS)
MESH = pl.DeviceIdType.MESH
F32 = jnp.float32
BF16 = jnp.bfloat16


def dot(a, b, dims, precision=None):
    return lax.dot_general(
        a, b, (dims, ((), ())), preferred_element_type=F32, precision=precision
    )


NN = ((1,), (0,))
NT = ((1,), (1,))
TN = ((0,), (0,))


def split3(x):
    high = x.astype(BF16)
    rest = x - high.astype(F32)
    mid = rest.astype(BF16)
    low = (rest - mid.astype(F32)).astype(BF16)
    return high, mid, low


def split2(x):
    high = x.astype(BF16)
    return high, (x - high.astype(F32)).astype(BF16)


def diagonal(rows):
    return lax.broadcasted_iota(jnp.int32, (rows, rows), 0) == lax.broadcasted_iota(
        jnp.int32, (rows, rows), 1
    )


def column_to_row(column):
    count = column.shape[0]
    pieces = []
    for first in range(0, count, 128):
        rows = min(128, count - first)
        piece = jnp.broadcast_to(column[first : first + rows], (rows, rows))
        pieces.append(jnp.sum(jnp.where(diagonal(rows), piece, 0.0), axis=0, keepdims=True))
    return jnp.concatenate(pieces, axis=1) if len(pieces) > 1 else pieces[0]


def row_to_column(row):
    count = row.shape[1]
    pieces = []
    for first in range(0, count, 128):
        rows = min(128, count - first)
        piece = jnp.broadcast_to(row[:, first : first + rows], (rows, rows))
        pieces.append(jnp.sum(jnp.where(diagonal(rows), piece, 0.0), axis=1, keepdims=True))
    return jnp.concatenate(pieces, axis=0) if len(pieces) > 1 else pieces[0]


def kernel(
    n,
    cashflows,
    trade_set_hbm,
    trade_end_hbm,
    spline_hbm,
    knots_hbm,
    factor_load_hbm,
    vol_hbm,
    start_state_hbm,
    normals_hbm,
    set_cpty_hbm,
    default_prob_hbm,
    base_value_hbm,
    later_adjoint_hbm,
    knot_hbm,
    alloc_hbm,
    start_hbm,
    trade_set,
    trade_end,
    spline,
    knots,
    factor_load,
    vol,
    start_state,
    normals,
    set_cpty,
    default_prob,
    base_value,
    later_adjoint,
    knot_out,
    alloc_out,
    start_out,
    flows,
    value_pair,
    value_sums,
    slope_pair,
    slope_sums,
    rate_pair,
    rate_sums,
    alloc_sent,
    alloc_pair,
    alloc_chip,
    alloc_sums,
    net,
    exact,
    features,
    values,
    adjoint,
    weighted,
    rate_acc,
    loading_rows,
    discount_rows,
    horizon_rows,
    weight_rows,
    load_split,
    exact_sums,
    load_sems,
    store_sems,
    send_sems,
    recv_sems,
):
    dates, factors, paths = normals.shape
    grid = knots.shape[1]
    trades = cashflows.shape[0]
    sets = base_value.shape[1]
    half = flows.shape[3] - sets
    chips = n // 2
    paths_all = paths * n
    me = lax.axis_index("path")
    chip, core = me // 2, me % 2
    partner = me + 1 - 2 * core

    loads = []
    for source, target in (
        (trade_set_hbm, trade_set),
        (trade_end_hbm, trade_end),
        (spline_hbm, spline),
        (knots_hbm, knots),
        (factor_load_hbm, factor_load),
        (vol_hbm, vol),
        (start_state_hbm, start_state),
        (normals_hbm, normals),
        (set_cpty_hbm, set_cpty),
        (default_prob_hbm, default_prob),
        (base_value_hbm, base_value),
        (later_adjoint_hbm, later_adjoint),
    ):
        loads.append(pltpu.make_async_copy(source, target, load_sems.at[len(loads)]))
        loads[-1].start()

    barrier = pltpu.get_barrier_semaphore()

    def greet(step, carry):
        pl.semaphore_signal(
            barrier, inc=1, device_id={"path": lax.rem(me + 2 * step, n)}, device_id_type=MESH
        )
        return carry

    lax.fori_loop(1, chips, greet, 0)
    pl.semaphore_signal(barrier, inc=1, device_id={"path": partner}, device_id_type=MESH)

    loads[0].wait()
    loads[1].wait()
    set_id = row_to_column(trade_set[...].astype(F32)).astype(jnp.int32)
    end = row_to_column(trade_end[...].astype(F32)).astype(jnp.int32)
    live = jnp.where(
        lax.broadcasted_iota(jnp.int32, (trades, grid), 1) < end,
        cashflows[...].astype(F32),
        0.0,
    )
    upper = jnp.concatenate(
        [live[:, half:], jnp.zeros((trades, 2 * half - grid), F32)], axis=1
    )
    one_hot = (lax.broadcasted_iota(jnp.int32, (trades, sets), 1) == set_id).astype(F32)
    message = jnp.concatenate(
        [
            jnp.concatenate([live[:, :half], upper], axis=0),
            jnp.concatenate([one_hot, one_hot], axis=0),
        ],
        axis=1,
    )
    flows[core, chip] = message.astype(BF16)

    pl.semaphore_wait(barrier, chips)

    def send_flows(step, carry):
        pltpu.make_async_remote_copy(
            src_ref=flows.at[core, chip],
            dst_ref=flows.at[core, chip],
            send_sem=send_sems.at[0],
            recv_sem=recv_sems.at[0],
            device_id={"path": lax.rem(me + 2 * step, n)},
            device_id_type=MESH,
        ).start()
        return carry

    lax.fori_loop(1, chips, send_flows, 0)

    def send_pair(buffer, target, which):
        copy = pltpu.make_async_remote_copy(
            src_ref=buffer,
            dst_ref=target,
            send_sem=send_sems.at[which],
            recv_sem=recv_sems.at[which],
            device_id={"path": partner},
            device_id_type=MESH,
        )
        copy.start()
        return copy

    def send_chips(source, buffer, which):
        def send(step, carry):
            other = lax.rem(chip + step, chips)
            pltpu.make_async_remote_copy(
                src_ref=source(other),
                dst_ref=buffer.at[chip],
                send_sem=send_sems.at[which],
                recv_sem=recv_sems.at[which],
                device_id={"path": 2 * other + core},
                device_id_type=MESH,
            ).start()
            return carry

        lax.fori_loop(1, chips, send, 0)

    def wait_chips(buffer, sems, which):
        others = buffer.at[pl.ds(0, chips - 1)]
        pltpu.make_async_copy(others, others, sems.at[which]).wait()

    def send_sum(pair, sums, which):
        sums[chip] = pair[0] + pair[1]
        send_chips(lambda other: sums.at[chip], sums, which)

    index = lax.broadcasted_iota(jnp.int32, (dates, grid), 1)
    date = lax.broadcasted_iota(jnp.int32, (dates, grid), 0)
    alive = 120 * (index + 1) > grid * (date + 1)
    maturity = HORIZON_YEARS * (index + 1).astype(F32) / grid
    fixing = STEP_YEARS * (date + 1).astype(F32)
    horizon = jnp.where(alive, maturity - fixing, 0.0)
    horizon_rows[...] = horizon
    loading_rows[...] = (1.0 - jnp.exp(-MEAN_REV * horizon)) / MEAN_REV
    for load in loads[2:]:
        load.wait()
    zero_rate = column_to_row(jnp.sum(spline[...] * knots[...], axis=1, keepdims=True))
    discount_rows[...] = jnp.where(alive, jnp.exp(-zero_rate * horizon), 0.0)

    counter = (
        lax.broadcasted_iota(jnp.int32, (default_prob.shape[1], sets), 0) == set_cpty[...]
    ).astype(F32)
    weight_rows[...] = LOSS_RATE * dot(
        default_prob[...], counter, NN, precision=lax.Precision.HIGHEST
    )

    high, mid, low = split3(factor_load[...])
    load_split[...] = jnp.concatenate([high, high, mid, high, mid, low], axis=0)

    def forward(i, state):
        here = lax.broadcasted_iota(jnp.int32, (1, dates), 1) == i
        date_vol = jnp.sum(jnp.where(here, vol[...], 0.0), axis=1, keepdims=True)
        state = DECAY * state + date_vol * normals[i]
        s_high, s_mid, s_low = split3(state)
        stacked = jnp.concatenate([s_high, s_mid, s_high, s_low, s_mid, s_high], axis=0)
        shift = dot(stacked, load_split[...], TN)
        bond = jnp.exp(-(loading_rows[pl.ds(i, 1), :] * shift))
        feat = discount_rows[pl.ds(i, 1), :] * bond
        exact[i] = feat
        features[i] = feat.astype(BF16)
        exact_sums[pl.ds(i, 1), :] = jnp.sum(feat, axis=0, keepdims=True)
        return state

    early = dates - dates // 4
    state = lax.fori_loop(0, early, forward, start_state[...])
    part = flows.at[0, pl.ds(0, chips - 1)]
    pltpu.make_async_copy(part, part, recv_sems.at[0]).wait()
    share = pltpu.make_async_remote_copy(
        src_ref=flows.at[core],
        dst_ref=flows.at[core],
        send_sem=send_sems.at[1],
        recv_sem=recv_sems.at[1],
        device_id={"path": partner},
        device_id_type=MESH,
    )
    share.start()
    lax.fori_loop(early, dates, forward, state)
    pltpu.make_async_copy(part, part, send_sems.at[0]).wait()
    share.wait()

    rows = n * 2 * trades
    all_flows = flows[:, :, :, :half].reshape(rows, half)
    member = flows[:, :, :, half:].reshape(rows, sets)
    is_upper = (lax.broadcasted_iota(jnp.int32, (rows, sets), 0) // trades) % 2 == 1
    member_wide = member.astype(F32)
    member_low = jnp.where(is_upper, 0.0, member_wide).astype(BF16)
    member_high = jnp.where(is_upper, member_wide, 0.0).astype(BF16)
    net[:, :half] = dot(member_low, all_flows, TN).astype(BF16)
    net[:, half:] = dot(member_high, all_flows, TN)[:, : grid - half].astype(BF16)

    def value(i, carry):
        found = dot(features[i], net[...], NT)
        values[i] = found
        value_pair[core, pl.ds(i, 1), :] = jnp.sum(found, axis=0, keepdims=True)
        return carry

    lax.fori_loop(0, dates, value, 0)
    send_pair(value_pair.at[core], value_pair.at[core], 2).wait()
    send_sum(value_pair, value_sums, 3)
    wait_chips(value_sums, recv_sems, 3)
    offset = base_value[...] - jnp.sum(value_sums[...], axis=0) / paths_all
    weights = weight_rows[...]
    for i in range(dates):
        shifted = values[i] + offset[i : i + 1]
        slope = weights[i : i + 1] * jax.nn.sigmoid(SHARPNESS * shifted)
        total = jnp.sum(slope, axis=0, keepdims=True)
        slope_pair[core, i : i + 1, :] = total
        adjoint[i * paths : (i + 1) * paths, :sets] = (slope - total / paths).astype(BF16)
    slope_copy = send_pair(slope_pair.at[core], slope_pair.at[core], 4)
    adjoint[:, sets:] = (
        lax.broadcasted_iota(jnp.int32, (dates * paths, 128), 0) // paths
        == lax.broadcasted_iota(jnp.int32, (dates * paths, 128), 1)
    ).astype(BF16)
    weighted[...] = jnp.zeros_like(weighted)
    rate_acc[...] = jnp.zeros_like(rate_acc)
    loading_rows[...] = loading_rows[...] * jnp.exp(
        lax.broadcasted_iota(jnp.int32, (dates, grid), 0).astype(F32)
        * (-MEAN_REV * STEP_YEARS)
    )

    def backward(i, carry):
        adj = adjoint[pl.ds(pl.multiple_of(i * paths, paths), paths), :sets]
        product = dot(adj, net[...], NN) * exact[i]
        weighted[...] += loading_rows[pl.ds(i, 1), :] * product
        folded = jnp.sum(product.reshape(paths // 8, 8, grid), axis=0)
        rate_acc[...] += horizon_rows[pl.ds(i, 1), :] * folded
        return carry

    lax.fori_loop(0, dates // 4, backward, 0)
    slope_copy.wait()
    send_sum(slope_pair, slope_sums, 5)
    lax.fori_loop(dates // 4, dates, backward, 0)
    sums = dot(adjoint[...], features[...].reshape(dates * paths, grid), TN)

    wait_chips(slope_sums, recv_sems, 5)
    remainder = slope_pair[core] / paths - jnp.sum(slope_sums[...], axis=0) / paths_all
    common = dot(jnp.concatenate(split2(remainder), axis=0), net[...], NN)
    common = common[:dates] + common[dates:]
    rate = jnp.sum(rate_acc[...], axis=0, keepdims=True) + jnp.sum(
        horizon_rows[...] * common * exact_sums[...], axis=0, keepdims=True
    )
    rate = rate * (-1.0 / paths_all)
    lines = rate_sums.shape[1]
    for line in range(lines):
        first = 128 * line
        if first < grid:
            piece = rate[:, first : first + 128]
            rate_pair[core, line : line + 1, : piece.shape[1]] = piece
            if piece.shape[1] < 128:
                rate_pair[core, line : line + 1, piece.shape[1] :] = jnp.zeros(
                    (1, 128 - piece.shape[1]), F32
                )
        else:
            rate_pair[core, line : line + 1, :] = jnp.zeros((1, 128), F32)
    rate_copy = send_pair(rate_pair.at[core], rate_pair.at[core], 6)

    sums = sums[:sets] + dot(
        remainder, sums[sets : sets + dates], TN, precision=lax.Precision.HIGHEST
    )
    sums = sums * (1.0 / paths_all)
    sums = jnp.concatenate([sums, jnp.zeros((sets, 2 * half - grid), F32)], axis=1)
    stacked = jnp.concatenate(split2(sums), axis=0)
    low_part = dot(all_flows, stacked[:, :half], NT)
    high_part = dot(all_flows, stacked[:, half:], NT)
    low_part = low_part[:, :sets] + low_part[:, sets:]
    high_part = high_part[:, :sets] + high_part[:, sets:]
    terms = jnp.where(is_upper, high_part, low_part) * member_wide
    terms = terms.reshape(2, chips, 2, trades, sets)
    alloc_sent[...] = terms[:, :, 0] + terms[:, :, 1]
    alloc_copy = send_pair(alloc_sent.at[1 - core], alloc_pair, 8)
    rate_copy.wait()
    send_sum(rate_pair, rate_sums, 7)

    loading_rows[...] = loading_rows[...] * common
    block = 32

    def add_common(step, carry):
        at = pl.ds(pl.multiple_of(step * block, block), block)
        held = weighted[at, :]
        for i in range(dates):
            held = held + loading_rows[i : i + 1, :] * exact[i, at, :]
        weighted[at, :] = held
        return carry

    lax.fori_loop(0, paths // block, add_common, 0)
    alloc_copy.wait()
    alloc_chip[...] = alloc_sent[core] + alloc_pair[...]
    alloc_sums[chip] = alloc_chip[chip]
    send_chips(lambda other: alloc_chip.at[other], alloc_sums, 9)

    load_high, load_low = split2(factor_load[...])
    y_high, y_low = split2(weighted[...])
    local = dot(jnp.concatenate([load_high, load_low], axis=0), y_high, NT)
    local = local[:factors] + local[factors:] + dot(load_high, y_low, NT)
    start_out[...] = DECAY**dates * later_adjoint[...] - DECAY * local
    start_store = pltpu.make_async_copy(start_out, start_hbm, store_sems.at[0])
    start_store.start()

    wait_chips(rate_sums, recv_sems, 7)
    total = jnp.sum(rate_sums[...], axis=0)
    column = row_to_column(
        jnp.concatenate([total[line : line + 1] for line in range(lines)], axis=1)[:, :grid]
    )
    knot_out[...] = jnp.sum(spline[...] * column, axis=0, keepdims=True)
    knot_store = pltpu.make_async_copy(knot_out, knot_hbm, store_sems.at[1])
    knot_store.start()

    wait_chips(alloc_sums, recv_sems, 9)
    alloc_out[...] = column_to_row(
        jnp.sum(jnp.sum(alloc_sums[...], axis=0), axis=1, keepdims=True)
    )
    alloc_store = pltpu.make_async_copy(alloc_out, alloc_hbm, store_sems.at[2])
    alloc_store.start()
    for buffer, which in ((value_sums, 3), (slope_sums, 5), (rate_sums, 7), (alloc_sums, 9)):
        wait_chips(buffer, send_sems, which)
    for store in (start_store, knot_store, alloc_store):
        store.wait()


def hand_on(knot_part, alloc_part, start_part, knot_out, alloc_out, start_out, sems):
    copies = []
    for source, target in (
        (start_part, start_out),
        (knot_part, knot_out),
        (alloc_part, alloc_out),
    ):
        copies.append(pltpu.make_async_copy(source, target, sems.at[len(copies)]))
        copies[-1].start()
    for copy in copies:
        copy.wait()


def per_device(
    normals,
    start_state,
    later_adjoint,
    vol,
    factor_load,
    knots,
    spline_jac,
    cashflows,
    trade_set,
    trade_end,
    set_cpty,
    default_prob,
    base_value,
):
    n = lax.axis_size("path")
    dates, factors, paths = normals.shape
    grid = knots.shape[0]
    trades = cashflows.shape[0]
    sets = base_value.shape[1]
    half = -(-grid // 256) * 128
    lines = -(-grid // 1024) * 8
    vmem = pl.BlockSpec(memory_space=pltpu.VMEM)
    hbm = pl.BlockSpec(memory_space=pltpu.HBM)
    arguments = (
        trade_set.reshape(1, trades),
        trade_end.reshape(1, trades),
        spline_jac,
        knots.reshape(1, grid),
        factor_load,
        vol.reshape(1, dates),
        start_state,
        normals,
        set_cpty.reshape(1, sets),
        default_prob,
        base_value,
        later_adjoint,
    )
    out_shape = [
        jax.ShapeDtypeStruct((1, grid), F32),
        jax.ShapeDtypeStruct((1, trades), F32),
        jax.ShapeDtypeStruct((factors, paths), F32),
    ]
    parts = pl.pallas_call(
        functools.partial(kernel, n),
        out_shape=out_shape,
        in_specs=[vmem] + [hbm] * len(arguments),
        out_specs=[hbm] * 3,
        scratch_shapes=[pltpu.VMEM(each.shape, each.dtype) for each in (*arguments, *out_shape)]
        + [
            pltpu.VMEM((2, n // 2, 2 * trades, half + sets), BF16),
            pltpu.VMEM((2, dates, sets), F32),
            pltpu.VMEM((n // 2, dates, sets), F32),
            pltpu.VMEM((2, dates, sets), F32),
            pltpu.VMEM((n // 2, dates, sets), F32),
            pltpu.VMEM((2, lines, 128), F32),
            pltpu.VMEM((n // 2, lines, 128), F32),
            pltpu.VMEM((2, n // 2, trades, sets), F32),
            pltpu.VMEM((n // 2, trades, sets), F32),
            pltpu.VMEM((n // 2, trades, sets), F32),
            pltpu.VMEM((n // 2, trades, sets), F32),
            pltpu.VMEM((sets, grid), BF16),
            pltpu.VMEM((dates, paths, grid), F32),
            pltpu.VMEM((dates, paths, grid), BF16),
            pltpu.VMEM((dates, paths, sets), F32),
            pltpu.VMEM((dates * paths, sets + 128), BF16),
            pltpu.VMEM((paths, grid), F32),
            pltpu.VMEM((8, grid), F32),
            pltpu.VMEM((dates, grid), F32),
            pltpu.VMEM((dates, grid), F32),
            pltpu.VMEM((dates, grid), F32),
            pltpu.VMEM((dates, sets), F32),
            pltpu.VMEM((6 * factors, grid), BF16),
            pltpu.VMEM((dates, grid), F32),
            pltpu.SemaphoreType.DMA((len(arguments),)),
            pltpu.SemaphoreType.DMA((3,)),
            pltpu.SemaphoreType.DMA((10,)),
            pltpu.SemaphoreType.DMA((10,)),
        ],
        compiler_params=pltpu.CompilerParams(
            collective_id=0, has_side_effects=True, vmem_limit_bytes=58 * 1024 * 1024
        ),
    )(cashflows, *arguments)
    knot_grad, alloc, start_adjoint = pl.pallas_call(
        hand_on,
        out_shape=out_shape,
        in_specs=[hbm] * 3,
        out_specs=[hbm] * 3,
        scratch_shapes=[pltpu.SemaphoreType.DMA((3,))],
        compiler_params=pltpu.CompilerParams(vmem_limit_bytes=58 * 1024 * 1024),
    )(*parts)
    return knot_grad.reshape(grid), alloc.reshape(trades), start_adjoint


def solution(mesh):
    in_specs = (
        P(None, None, ("group", "path")),
        P(None, ("group", "path")),
        P(None, ("group", "path")),
        P(),
        P(),
        P(),
        P(),
        P(("group", "path"), None),
        P(("group", "path"), None),
        P(("group", "path")),
        P("group", None),
        P(),
        P(None, "group"),
    )
    out_specs = (P("group"), P(("group", "path")), P(None, ("group", "path")))
    return jax.shard_map(
        per_device, mesh=mesh, in_specs=in_specs, out_specs=out_specs, check_vma=False
    )
```

```python
import functools
import math

import jax
import jax.numpy as jnp
from jax import lax
from jax.experimental import pallas as pl
from jax.experimental.pallas import tpu as pltpu
from jax.sharding import PartitionSpec as P

MEAN_REV = 0.05
STEP_YEARS = 0.25
HORIZON_YEARS = 30.0
SHARPNESS = 4.0
LOSS_RATE = 0.6
DECAY = math.exp(-MEAN_REV * STEP_YEARS)
MESH = pl.DeviceIdType.MESH
F32 = jnp.float32
BF16 = jnp.bfloat16


def dot(a, b, dims, precision=None):
    return lax.dot_general(
        a, b, (dims, ((), ())), preferred_element_type=F32, precision=precision
    )


NN = ((1,), (0,))
NT = ((1,), (1,))
TN = ((0,), (0,))


def split3(x):
    high = x.astype(BF16)
    rest = x - high.astype(F32)
    mid = rest.astype(BF16)
    low = (rest - mid.astype(F32)).astype(BF16)
    return high, mid, low


def split2(x):
    high = x.astype(BF16)
    return high, (x - high.astype(F32)).astype(BF16)


def diagonal(rows):
    return lax.broadcasted_iota(jnp.int32, (rows, rows), 0) == lax.broadcasted_iota(
        jnp.int32, (rows, rows), 1
    )


def column_to_row(column):
    count = column.shape[0]
    pieces = []
    for first in range(0, count, 128):
        rows = min(128, count - first)
        piece = jnp.broadcast_to(column[first : first + rows], (rows, rows))
        pieces.append(jnp.sum(jnp.where(diagonal(rows), piece, 0.0), axis=0, keepdims=True))
    return jnp.concatenate(pieces, axis=1) if len(pieces) > 1 else pieces[0]


def row_to_column(row):
    count = row.shape[1]
    pieces = []
    for first in range(0, count, 128):
        rows = min(128, count - first)
        piece = jnp.broadcast_to(row[:, first : first + rows], (rows, rows))
        pieces.append(jnp.sum(jnp.where(diagonal(rows), piece, 0.0), axis=1, keepdims=True))
    return jnp.concatenate(pieces, axis=0) if len(pieces) > 1 else pieces[0]


def kernel(
    n,
    cashflows,
    trade_set_hbm,
    trade_end_hbm,
    spline_hbm,
    knots_hbm,
    factor_load_hbm,
    vol_hbm,
    start_state_hbm,
    normals_hbm,
    set_cpty_hbm,
    default_prob_hbm,
    base_value_hbm,
    later_adjoint_hbm,
    knot_hbm,
    alloc_hbm,
    start_hbm,
    trade_set,
    trade_end,
    spline,
    knots,
    factor_load,
    vol,
    start_state,
    normals,
    set_cpty,
    default_prob,
    base_value,
    later_adjoint,
    knot_out,
    alloc_out,
    start_out,
    flows,
    value_pair,
    value_sums,
    slope_pair,
    slope_sums,
    rate_pair,
    rate_sums,
    alloc_sent,
    alloc_pair,
    alloc_chip,
    alloc_sums,
    net,
    exact,
    features,
    values,
    adjoint,
    weighted,
    rate_acc,
    loading_rows,
    discount_rows,
    horizon_rows,
    weight_rows,
    load_split,
    exact_sums,
    feature_sums,
    load_sems,
    store_sems,
    send_sems,
    recv_sems,
):
    dates, factors, paths = normals.shape
    grid = knots.shape[1]
    trades = cashflows.shape[0]
    sets = base_value.shape[1]
    half = flows.shape[3] - sets
    chips = n // 2
    paths_all = paths * n
    me = lax.axis_index("path")
    chip, core = me // 2, me % 2
    partner = me + 1 - 2 * core

    loads = []
    for source, target in (
        (trade_set_hbm, trade_set),
        (trade_end_hbm, trade_end),
        (spline_hbm, spline),
        (knots_hbm, knots),
        (factor_load_hbm, factor_load),
        (vol_hbm, vol),
        (start_state_hbm, start_state),
        (normals_hbm, normals),
        (set_cpty_hbm, set_cpty),
        (default_prob_hbm, default_prob),
        (base_value_hbm, base_value),
        (later_adjoint_hbm, later_adjoint),
    ):
        loads.append(pltpu.make_async_copy(source, target, load_sems.at[len(loads)]))
        loads[-1].start()

    barrier = pltpu.get_barrier_semaphore()

    def greet(step, carry):
        pl.semaphore_signal(
            barrier, inc=1, device_id={"path": lax.rem(me + 2 * step, n)}, device_id_type=MESH
        )
        return carry

    lax.fori_loop(1, chips, greet, 0)
    pl.semaphore_signal(barrier, inc=1, device_id={"path": partner}, device_id_type=MESH)

    loads[0].wait()
    loads[1].wait()
    set_id = row_to_column(trade_set[...].astype(F32)).astype(jnp.int32)
    end = row_to_column(trade_end[...].astype(F32)).astype(jnp.int32)
    live = jnp.where(
        lax.broadcasted_iota(jnp.int32, (trades, grid), 1) < end,
        cashflows[...].astype(F32),
        0.0,
    )
    upper = jnp.concatenate(
        [live[:, half:], jnp.zeros((trades, 2 * half - grid), F32)], axis=1
    )
    one_hot = (lax.broadcasted_iota(jnp.int32, (trades, sets), 1) == set_id).astype(F32)
    message = jnp.concatenate(
        [
            jnp.concatenate([live[:, :half], upper], axis=0),
            jnp.concatenate([one_hot, one_hot], axis=0),
        ],
        axis=1,
    )
    flows[core, chip] = message.astype(BF16)

    pl.semaphore_wait(barrier, chips)

    def send_flows(step, carry):
        pltpu.make_async_remote_copy(
            src_ref=flows.at[core, chip],
            dst_ref=flows.at[core, chip],
            send_sem=send_sems.at[0],
            recv_sem=recv_sems.at[0],
            device_id={"path": lax.rem(me + 2 * step, n)},
            device_id_type=MESH,
        ).start()
        return carry

    lax.fori_loop(1, chips, send_flows, 0)

    def send_pair(buffer, target, which):
        copy = pltpu.make_async_remote_copy(
            src_ref=buffer,
            dst_ref=target,
            send_sem=send_sems.at[which],
            recv_sem=recv_sems.at[which],
            device_id={"path": partner},
            device_id_type=MESH,
        )
        copy.start()
        return copy

    def send_chips(source, buffer, which):
        def send(step, carry):
            other = lax.rem(chip + step, chips)
            pltpu.make_async_remote_copy(
                src_ref=source(other),
                dst_ref=buffer.at[chip],
                send_sem=send_sems.at[which],
                recv_sem=recv_sems.at[which],
                device_id={"path": 2 * other + core},
                device_id_type=MESH,
            ).start()
            return carry

        lax.fori_loop(1, chips, send, 0)

    def wait_chips(buffer, sems, which):
        others = buffer.at[pl.ds(0, chips - 1)]
        pltpu.make_async_copy(others, others, sems.at[which]).wait()

    def send_sum(pair, sums, which):
        sums[chip] = pair[0] + pair[1]
        send_chips(lambda other: sums.at[chip], sums, which)

    index = lax.broadcasted_iota(jnp.int32, (dates, grid), 1)
    date = lax.broadcasted_iota(jnp.int32, (dates, grid), 0)
    alive = 120 * (index + 1) > grid * (date + 1)
    maturity = HORIZON_YEARS * (index + 1).astype(F32) / grid
    fixing = STEP_YEARS * (date + 1).astype(F32)
    horizon = jnp.where(alive, maturity - fixing, 0.0)
    horizon_rows[...] = horizon
    loading_rows[...] = -((1.0 - jnp.exp(-MEAN_REV * horizon)) / MEAN_REV)
    for load in loads[2:]:
        load.wait()
    pieces = [slice(first, min(first + 128, grid)) for first in range(0, grid, 128)]
    zero_rows = []
    for rows_at in pieces:
        full = [at for at in pieces if at.stop - at.start == 128]
        held = spline[rows_at, full[0]] * knots[:, full[0]]
        for at in full[1:]:
            held = held + spline[rows_at, at] * knots[:, at]
        column = jnp.sum(held, axis=1, keepdims=True)
        if len(full) < len(pieces):
            at = pieces[-1]
            column = column + jnp.sum(spline[rows_at, at] * knots[:, at], axis=1, keepdims=True)
        zero_rows.append(column_to_row(column))
    zero_rate = jnp.concatenate(zero_rows, axis=1)
    discount_rows[...] = jnp.where(alive, jnp.exp(-zero_rate * horizon), 0.0)

    counter = (
        lax.broadcasted_iota(jnp.int32, (default_prob.shape[1], sets), 0) == set_cpty[...]
    ).astype(F32)
    weight_rows[...] = LOSS_RATE * dot(
        default_prob[...], counter, NN, precision=lax.Precision.HIGHEST
    )

    high, mid, low = split3(factor_load[...])
    load_split[...] = jnp.concatenate([high, high, mid, high, mid, low], axis=0)

    def forward(i, state):
        here = lax.broadcasted_iota(jnp.int32, (1, dates), 1) == i
        date_vol = jnp.sum(jnp.where(here, vol[...], 0.0), axis=1, keepdims=True)
        state = DECAY * state + date_vol * normals[i]
        s_high, s_mid, s_low = [part.astype(F32) for part in split3(state)]
        stacked = jnp.concatenate([s_high, s_mid, s_high, s_low, s_mid, s_high], axis=0)
        stacked = stacked.T.astype(BF16)
        date = pl.ds(i, 1)
        discount_row, loading_row = discount_rows[date, :], loading_rows[date, :]
        exact_row, feature_row = [], []
        for at in pieces:
            shift = dot(stacked, load_split[:, at], NN)
            feat = discount_row[:, at] * jnp.exp(loading_row[:, at] * shift)
            rounded = feat.astype(BF16)
            exact[i, :, at] = feat
            features[i, :, at] = rounded
            exact_row.append(jnp.sum(feat, axis=0, keepdims=True))
            feature_row.append(jnp.sum(rounded.astype(F32), axis=0, keepdims=True))
        exact_sums[date, :] = jnp.concatenate(exact_row, axis=1)
        feature_sums[date, :] = jnp.concatenate(feature_row, axis=1)
        return state

    early = dates - dates // 4
    state = lax.fori_loop(0, early, forward, start_state[...])
    part = flows.at[0, pl.ds(0, chips - 1)]
    pltpu.make_async_copy(part, part, recv_sems.at[0]).wait()
    share = pltpu.make_async_remote_copy(
        src_ref=flows.at[core],
        dst_ref=flows.at[core],
        send_sem=send_sems.at[1],
        recv_sem=recv_sems.at[1],
        device_id={"path": partner},
        device_id_type=MESH,
    )
    share.start()
    lax.fori_loop(early, dates, forward, state)
    pltpu.make_async_copy(part, part, send_sems.at[0]).wait()
    share.wait()

    rows = n * 2 * trades
    all_flows = flows[:, :, :, :half].reshape(rows, half)
    member = flows[:, :, :, half:].reshape(rows, sets)
    is_upper = (lax.broadcasted_iota(jnp.int32, (rows, sets), 0) // trades) % 2 == 1
    member_wide = member.astype(F32)
    member_low = jnp.where(is_upper, 0.0, member_wide).astype(BF16)
    member_high = jnp.where(is_upper, member_wide, 0.0).astype(BF16)
    net[:, :half] = dot(member_low, all_flows, TN).astype(BF16)
    net[:, half:] = dot(member_high, all_flows, TN)[:, : grid - half].astype(BF16)

    def value(i, carry):
        found = dot(features[i], net[...], NT)
        values[i] = found
        value_pair[core, pl.ds(i, 1), :] = jnp.sum(found, axis=0, keepdims=True)
        return carry

    lax.fori_loop(0, dates, value, 0)
    send_pair(value_pair.at[core], value_pair.at[core], 2).wait()
    send_sum(value_pair, value_sums, 3)
    wait_chips(value_sums, recv_sems, 3)
    offset = base_value[...] - jnp.sum(value_sums[...], axis=0) / paths_all
    weights = weight_rows[...]
    for i in range(dates):
        shifted = values[i] + offset[i : i + 1]
        slope = weights[i : i + 1] * jax.nn.sigmoid(SHARPNESS * shifted)
        total = jnp.sum(slope, axis=0, keepdims=True)
        slope_pair[core, i : i + 1, :] = total
        adjoint[i * paths : (i + 1) * paths, :] = (slope - total / paths).astype(BF16)
    slope_copy = send_pair(slope_pair.at[core], slope_pair.at[core], 4)
    weighted[...] = jnp.zeros_like(weighted)
    rate_acc[...] = jnp.zeros_like(rate_acc)
    loading_rows[...] = loading_rows[...] * jnp.exp(
        lax.broadcasted_iota(jnp.int32, (dates, grid), 0).astype(F32)
        * (-MEAN_REV * STEP_YEARS)
    )

    def backward(i, carry):
        adj = adjoint[pl.ds(pl.multiple_of(i * paths, paths), paths), :]
        date = pl.ds(i, 1)
        loading_row, horizon_row = loading_rows[date, :], horizon_rows[date, :]
        for at in pieces:
            product = dot(adj, net[:, at], NN) * exact[i, :, at]
            weighted[:, at] += loading_row[:, at] * product
            folded = jnp.sum(product.reshape(paths // 8, 8, at.stop - at.start), axis=0)
            rate_acc[:, at] += horizon_row[:, at] * folded
        return carry

    lax.fori_loop(0, dates // 4, backward, 0)
    slope_copy.wait()
    send_sum(slope_pair, slope_sums, 5)
    lax.fori_loop(dates // 4, dates, backward, 0)
    sums = dot(adjoint[...], features[...].reshape(dates * paths, grid), TN)

    wait_chips(slope_sums, recv_sems, 5)
    remainder = slope_pair[core] / paths - jnp.sum(slope_sums[...], axis=0) / paths_all
    common = dot(jnp.concatenate(split2(remainder), axis=0), net[...], NN)
    common = common[:dates] + common[dates:]
    rate = jnp.sum(rate_acc[...], axis=0, keepdims=True) + jnp.sum(
        horizon_rows[...] * common * exact_sums[...], axis=0, keepdims=True
    )
    rate = rate * (-1.0 / paths_all)
    lines = rate_sums.shape[1]
    for line in range(lines):
        first = 128 * line
        if first < grid:
            piece = rate[:, first : first + 128]
            rate_pair[core, line : line + 1, : piece.shape[1]] = piece
            if piece.shape[1] < 128:
                rate_pair[core, line : line + 1, piece.shape[1] :] = jnp.zeros(
                    (1, 128 - piece.shape[1]), F32
                )
        else:
            rate_pair[core, line : line + 1, :] = jnp.zeros((1, 128), F32)
    rate_copy = send_pair(rate_pair.at[core], rate_pair.at[core], 6)

    sums = sums + dot(remainder, feature_sums[...], TN, precision=lax.Precision.HIGHEST)
    sums = sums * (1.0 / paths_all)
    sums = jnp.concatenate([sums, jnp.zeros((sets, 2 * half - grid), F32)], axis=1)
    stacked = jnp.concatenate(split2(sums), axis=0)
    low_part = dot(all_flows, stacked[:, :half], NT)
    high_part = dot(all_flows, stacked[:, half:], NT)
    low_part = low_part[:, :sets] + low_part[:, sets:]
    high_part = high_part[:, :sets] + high_part[:, sets:]
    terms = jnp.where(is_upper, high_part, low_part) * member_wide
    terms = terms.reshape(2, chips, 2, trades, sets)
    alloc_sent[...] = terms[:, :, 0] + terms[:, :, 1]
    alloc_copy = send_pair(alloc_sent.at[1 - core], alloc_pair, 8)
    rate_copy.wait()
    send_sum(rate_pair, rate_sums, 7)

    loading_rows[...] = loading_rows[...] * common
    alloc_copy.wait()
    alloc_chip[...] = alloc_sent[core] + alloc_pair[...]
    alloc_sums[chip] = alloc_chip[chip]
    send_chips(lambda other: alloc_chip.at[other], alloc_sums, 9)

    load_high, load_low = split2(factor_load[...])
    load_both = jnp.concatenate([load_high, load_low], axis=0)
    local = jnp.zeros((factors, paths), F32)
    for at in pieces:
        held = weighted[:, at]
        for i in range(dates):
            held = held + loading_rows[i : i + 1, at] * exact[i, :, at]
        y_high, y_low = split2(held)
        both = dot(load_both[:, at], y_high, NT)
        local = local + (both[:factors] + both[factors:] + dot(load_high[:, at], y_low, NT))
    start_out[...] = DECAY**dates * later_adjoint[...] + DECAY * local
    start_store = pltpu.make_async_copy(start_out, start_hbm, store_sems.at[0])
    start_store.start()

    wait_chips(rate_sums, recv_sems, 7)
    total = jnp.sum(rate_sums[...], axis=0)
    held = [None] * len(pieces)
    for line, rows_at in enumerate(pieces):
        count = rows_at.stop - rows_at.start
        column = row_to_column(total[line : line + 1, :count])
        for k, at in enumerate(pieces):
            product = spline[rows_at, at] * column
            product = jnp.sum(product.reshape(count // 8, 8, at.stop - at.start), axis=0)
            held[k] = product if line == 0 else held[k] + product
    for k, at in enumerate(pieces):
        knot_out[:, at] = jnp.sum(held[k], axis=0, keepdims=True)
    knot_store = pltpu.make_async_copy(knot_out, knot_hbm, store_sems.at[1])
    knot_store.start()

    wait_chips(alloc_sums, recv_sems, 9)
    alloc_out[...] = column_to_row(
        jnp.sum(jnp.sum(alloc_sums[...], axis=0), axis=1, keepdims=True)
    )
    alloc_store = pltpu.make_async_copy(alloc_out, alloc_hbm, store_sems.at[2])
    alloc_store.start()
    for buffer, which in ((value_sums, 3), (slope_sums, 5), (rate_sums, 7), (alloc_sums, 9)):
        wait_chips(buffer, send_sems, which)
    for store in (start_store, knot_store, alloc_store):
        store.wait()


def hand_on(knot_part, alloc_part, start_part, knot_out, alloc_out, start_out, sems):
    copies = []
    for source, target in (
        (start_part, start_out),
        (knot_part, knot_out),
        (alloc_part, alloc_out),
    ):
        copies.append(pltpu.make_async_copy(source, target, sems.at[len(copies)]))
        copies[-1].start()
    for copy in copies:
        copy.wait()


def per_device(
    normals,
    start_state,
    later_adjoint,
    vol,
    factor_load,
    knots,
    spline_jac,
    cashflows,
    trade_set,
    trade_end,
    set_cpty,
    default_prob,
    base_value,
):
    n = lax.axis_size("path")
    dates, factors, paths = normals.shape
    grid = knots.shape[0]
    trades = cashflows.shape[0]
    sets = base_value.shape[1]
    half = -(-grid // 256) * 128
    lines = -(-grid // 1024) * 8
    vmem = pl.BlockSpec(memory_space=pltpu.VMEM)
    hbm = pl.BlockSpec(memory_space=pltpu.HBM)
    arguments = (
        trade_set.reshape(1, trades),
        trade_end.reshape(1, trades),
        spline_jac,
        knots.reshape(1, grid),
        factor_load,
        vol.reshape(1, dates),
        start_state,
        normals,
        set_cpty.reshape(1, sets),
        default_prob,
        base_value,
        later_adjoint,
    )
    out_shape = [
        jax.ShapeDtypeStruct((1, grid), F32),
        jax.ShapeDtypeStruct((1, trades), F32),
        jax.ShapeDtypeStruct((factors, paths), F32),
    ]
    parts = pl.pallas_call(
        functools.partial(kernel, n),
        out_shape=out_shape,
        in_specs=[vmem] + [hbm] * len(arguments),
        out_specs=[hbm] * 3,
        scratch_shapes=[pltpu.VMEM(each.shape, each.dtype) for each in (*arguments, *out_shape)]
        + [
            pltpu.VMEM((2, n // 2, 2 * trades, half + sets), BF16),
            pltpu.VMEM((2, dates, sets), F32),
            pltpu.VMEM((n // 2, dates, sets), F32),
            pltpu.VMEM((2, dates, sets), F32),
            pltpu.VMEM((n // 2, dates, sets), F32),
            pltpu.VMEM((2, lines, 128), F32),
            pltpu.VMEM((n // 2, lines, 128), F32),
            pltpu.VMEM((2, n // 2, trades, sets), F32),
            pltpu.VMEM((n // 2, trades, sets), F32),
            pltpu.VMEM((n // 2, trades, sets), F32),
            pltpu.VMEM((n // 2, trades, sets), F32),
            pltpu.VMEM((sets, grid), BF16),
            pltpu.VMEM((dates, paths, grid), F32),
            pltpu.VMEM((dates, paths, grid), BF16),
            pltpu.VMEM((dates, paths, sets), F32),
            pltpu.VMEM((dates * paths, sets), BF16),
            pltpu.VMEM((paths, grid), F32),
            pltpu.VMEM((8, grid), F32),
            pltpu.VMEM((dates, grid), F32),
            pltpu.VMEM((dates, grid), F32),
            pltpu.VMEM((dates, grid), F32),
            pltpu.VMEM((dates, sets), F32),
            pltpu.VMEM((6 * factors, grid), BF16),
            pltpu.VMEM((dates, grid), F32),
            pltpu.VMEM((dates, grid), F32),
            pltpu.SemaphoreType.DMA((len(arguments),)),
            pltpu.SemaphoreType.DMA((3,)),
            pltpu.SemaphoreType.DMA((10,)),
            pltpu.SemaphoreType.DMA((10,)),
        ],
        compiler_params=pltpu.CompilerParams(
            collective_id=0, has_side_effects=True, vmem_limit_bytes=58 * 1024 * 1024
        ),
    )(cashflows, *arguments)
    knot_grad, alloc, start_adjoint = pl.pallas_call(
        hand_on,
        out_shape=out_shape,
        in_specs=[hbm] * 3,
        out_specs=[hbm] * 3,
        scratch_shapes=[pltpu.SemaphoreType.DMA((3,))],
        compiler_params=pltpu.CompilerParams(vmem_limit_bytes=58 * 1024 * 1024),
    )(*parts)
    return knot_grad.reshape(grid), alloc.reshape(trades), start_adjoint


def solution(mesh):
    in_specs = (
        P(None, None, ("group", "path")),
        P(None, ("group", "path")),
        P(None, ("group", "path")),
        P(),
        P(),
        P(),
        P(),
        P(("group", "path"), None),
        P(("group", "path"), None),
        P(("group", "path")),
        P("group", None),
        P(),
        P(None, "group"),
    )
    out_specs = (P("group"), P(("group", "path")), P(None, ("group", "path")))
    return jax.shard_map(
        per_device, mesh=mesh, in_specs=in_specs, out_specs=out_specs, check_vma=False
    )
```

```python
import functools
import math

import jax
import jax.numpy as jnp
from jax import lax
from jax.experimental import pallas as pl
from jax.experimental.pallas import tpu as pltpu
from jax.sharding import PartitionSpec as P

MEAN_REV = 0.05
STEP_YEARS = 0.25
HORIZON_YEARS = 30.0
SHARPNESS = 4.0
LOSS_RATE = 0.6
DECAY = math.exp(-MEAN_REV * STEP_YEARS)
MESH = pl.DeviceIdType.MESH
F32 = jnp.float32
BF16 = jnp.bfloat16


def dot(a, b, dims, precision=None):
    return lax.dot_general(
        a, b, (dims, ((), ())), preferred_element_type=F32, precision=precision
    )


NN = ((1,), (0,))
NT = ((1,), (1,))
TN = ((0,), (0,))


def split3(x):
    high = x.astype(BF16)
    rest = x - high.astype(F32)
    mid = rest.astype(BF16)
    low = (rest - mid.astype(F32)).astype(BF16)
    return high, mid, low


def split2(x):
    high = x.astype(BF16)
    return high, (x - high.astype(F32)).astype(BF16)


def diagonal(rows):
    return lax.broadcasted_iota(jnp.int32, (rows, rows), 0) == lax.broadcasted_iota(
        jnp.int32, (rows, rows), 1
    )


def column_to_row(column):
    count = column.shape[0]
    pieces = []
    for first in range(0, count, 128):
        rows = min(128, count - first)
        piece = jnp.broadcast_to(column[first : first + rows], (rows, rows))
        pieces.append(jnp.sum(jnp.where(diagonal(rows), piece, 0.0), axis=0, keepdims=True))
    return jnp.concatenate(pieces, axis=1) if len(pieces) > 1 else pieces[0]


def row_to_column(row):
    count = row.shape[1]
    pieces = []
    for first in range(0, count, 128):
        rows = min(128, count - first)
        piece = jnp.broadcast_to(row[:, first : first + rows], (rows, rows))
        pieces.append(jnp.sum(jnp.where(diagonal(rows), piece, 0.0), axis=1, keepdims=True))
    return jnp.concatenate(pieces, axis=0) if len(pieces) > 1 else pieces[0]


def kernel(
    n,
    cashflows,
    trade_set_hbm,
    trade_end_hbm,
    spline_hbm,
    knots_hbm,
    factor_load_hbm,
    vol_hbm,
    start_state_hbm,
    normals_hbm,
    set_cpty_hbm,
    default_prob_hbm,
    base_value_hbm,
    later_adjoint_hbm,
    knot_out,
    alloc_out,
    start_out,
    trade_set,
    trade_end,
    spline,
    knots,
    factor_load,
    vol,
    start_state,
    normals,
    set_cpty,
    default_prob,
    base_value,
    later_adjoint,
    flows,
    value_pair,
    value_sums,
    slope_pair,
    slope_sums,
    rate_pair,
    rate_sums,
    alloc_sent,
    alloc_pair,
    alloc_chip,
    alloc_sums,
    net,
    exact,
    features,
    values,
    adjoint,
    weighted,
    rate_acc,
    loading_rows,
    discount_rows,
    horizon_rows,
    weight_rows,
    load_split,
    exact_sums,
    feature_sums,
    load_sems,
    send_sems,
    recv_sems,
):
    dates, factors, paths = normals.shape
    grid = knots.shape[1]
    trades = cashflows.shape[0]
    sets = base_value.shape[1]
    half = flows.shape[3]
    chips = n // 2
    short = chips <= 16
    paths_all = paths * n
    me = lax.axis_index("path")
    chip, core = me // 2, me % 2
    partner = me + 1 - 2 * core

    loads = []
    for source, target in (
        (trade_set_hbm, trade_set),
        (trade_end_hbm, trade_end),
        (spline_hbm, spline),
        (knots_hbm, knots),
        (factor_load_hbm, factor_load),
        (vol_hbm, vol),
        (start_state_hbm, start_state),
        (normals_hbm, normals),
        (set_cpty_hbm, set_cpty),
        (default_prob_hbm, default_prob),
        (base_value_hbm, base_value),
        (later_adjoint_hbm, later_adjoint),
    ):
        loads.append(pltpu.make_async_copy(source, target, load_sems.at[len(loads)]))
        loads[-1].start()

    barrier = pltpu.get_barrier_semaphore()

    def greet(step, carry):
        pl.semaphore_signal(
            barrier, inc=1, device_id={"path": lax.rem(me + 2 * step, n)}, device_id_type=MESH
        )
        return carry

    lax.fori_loop(1, chips, greet, 0, unroll=short)
    pl.semaphore_signal(barrier, inc=1, device_id={"path": partner}, device_id_type=MESH)

    loads[0].wait()
    loads[1].wait()
    set_id = row_to_column(trade_set[...].astype(F32)).astype(jnp.int32)
    end = row_to_column(trade_end[...].astype(F32)).astype(jnp.int32)
    live = jnp.where(
        lax.broadcasted_iota(jnp.int32, (trades, grid), 1) < end,
        cashflows[...].astype(F32),
        0.0,
    )
    upper = jnp.concatenate(
        [
            live[:, half:],
            jnp.zeros((trades, 2 * half - grid - 2), F32),
            (set_id // 128).astype(F32),
            (set_id % 128).astype(F32),
        ],
        axis=1,
    )
    flows[core, chip] = jnp.concatenate([live[:, :half], upper], axis=0).astype(BF16)

    pl.semaphore_wait(barrier, chips)

    def send_flows(step, carry):
        pltpu.make_async_remote_copy(
            src_ref=flows.at[core, chip],
            dst_ref=flows.at[core, chip],
            send_sem=send_sems.at[0],
            recv_sem=recv_sems.at[0],
            device_id={"path": lax.rem(me + 2 * step, n)},
            device_id_type=MESH,
        ).start()
        return carry

    lax.fori_loop(1, chips, send_flows, 0, unroll=short)

    def send_pair(buffer, target, which):
        copy = pltpu.make_async_remote_copy(
            src_ref=buffer,
            dst_ref=target,
            send_sem=send_sems.at[which],
            recv_sem=recv_sems.at[which],
            device_id={"path": partner},
            device_id_type=MESH,
        )
        copy.start()
        return copy

    def send_chips(source, buffer, which):
        def send(step, carry):
            other = lax.rem(chip + step, chips)
            pltpu.make_async_remote_copy(
                src_ref=source(other),
                dst_ref=buffer.at[chip],
                send_sem=send_sems.at[which],
                recv_sem=recv_sems.at[which],
                device_id={"path": 2 * other + core},
                device_id_type=MESH,
            ).start()
            return carry

        lax.fori_loop(1, chips, send, 0, unroll=short)

    def wait_chips(buffer, sems, which):
        others = buffer.at[pl.ds(0, chips - 1)]
        pltpu.make_async_copy(others, others, sems.at[which]).wait()

    def send_sum(pair, sums, which):
        sums[chip] = pair[0] + pair[1]
        send_chips(lambda other: sums.at[chip], sums, which)

    index = lax.broadcasted_iota(jnp.int32, (dates, grid), 1)
    date = lax.broadcasted_iota(jnp.int32, (dates, grid), 0)
    alive = 120 * (index + 1) > grid * (date + 1)
    maturity = HORIZON_YEARS * (index + 1).astype(F32) / grid
    fixing = STEP_YEARS * (date + 1).astype(F32)
    horizon = jnp.where(alive, maturity - fixing, 0.0)
    horizon_rows[...] = horizon
    loading_rows[...] = -((1.0 - jnp.exp(-MEAN_REV * horizon)) / MEAN_REV)
    for load in loads[2:]:
        load.wait()
    pieces = [slice(first, min(first + 128, grid)) for first in range(0, grid, 128)]
    zero_rows = []
    for rows_at in pieces:
        full = [at for at in pieces if at.stop - at.start == 128]
        held = spline[rows_at, full[0]] * knots[:, full[0]]
        for at in full[1:]:
            held = held + spline[rows_at, at] * knots[:, at]
        column = jnp.sum(held, axis=1, keepdims=True)
        if len(full) < len(pieces):
            at = pieces[-1]
            column = column + jnp.sum(spline[rows_at, at] * knots[:, at], axis=1, keepdims=True)
        zero_rows.append(column_to_row(column))
    zero_rate = jnp.concatenate(zero_rows, axis=1)
    discount_rows[...] = jnp.where(alive, jnp.exp(-zero_rate * horizon), 0.0)

    counter = (
        lax.broadcasted_iota(jnp.int32, (default_prob.shape[1], sets), 0) == set_cpty[...]
    ).astype(F32)
    weight_rows[...] = LOSS_RATE * dot(
        default_prob[...], counter, NN, precision=lax.Precision.HIGHEST
    )

    high, mid, low = split3(factor_load[...])
    load_split[...] = jnp.concatenate([high, high, mid, high, mid, low], axis=0)

    def forward(i, state):
        here = lax.broadcasted_iota(jnp.int32, (1, dates), 1) == i
        date_vol = jnp.sum(jnp.where(here, vol[...], 0.0), axis=1, keepdims=True)
        state = DECAY * state + date_vol * normals[i]
        s_high, s_mid, s_low = [part.astype(F32) for part in split3(state)]
        stacked = jnp.concatenate([s_high, s_mid, s_high, s_low, s_mid, s_high], axis=0)
        stacked = stacked.T.astype(BF16)
        date = pl.ds(i, 1)
        discount_row, loading_row = discount_rows[date, :], loading_rows[date, :]
        exact_row, feature_row = [], []
        for at in pieces:
            shift = dot(stacked, load_split[:, at], NN)
            feat = discount_row[:, at] * jnp.exp(loading_row[:, at] * shift)
            rounded = feat.astype(BF16)
            exact[i, :, at] = feat
            features[i, :, at] = rounded
            exact_row.append(jnp.sum(feat, axis=0, keepdims=True))
            feature_row.append(jnp.sum(rounded.astype(F32), axis=0, keepdims=True))
        exact_sums[date, :] = jnp.concatenate(exact_row, axis=1)
        feature_sums[date, :] = jnp.concatenate(feature_row, axis=1)
        return state

    early = dates - dates // 4
    state = lax.fori_loop(0, early, forward, start_state[...])
    part = flows.at[0, pl.ds(0, chips - 1)]
    pltpu.make_async_copy(part, part, recv_sems.at[0]).wait()
    share = pltpu.make_async_remote_copy(
        src_ref=flows.at[core],
        dst_ref=flows.at[core],
        send_sem=send_sems.at[1],
        recv_sem=recv_sems.at[1],
        device_id={"path": partner},
        device_id_type=MESH,
    )
    share.start()
    lax.fori_loop(early, dates, forward, state)
    pltpu.make_async_copy(part, part, send_sems.at[0]).wait()
    share.wait()

    rows = n * 2 * trades
    all_flows = flows[...].reshape(rows, half)
    tail = flows[:, :, :, half - 128 :].astype(F32).reshape(n, 2 * trades, 128)
    tail = tail[:, trades:].reshape(n * trades, 128)
    all_sets = (128.0 * tail[:, 126:127] + tail[:, 127:128]).astype(jnp.int32)
    member = lax.broadcasted_iota(jnp.int32, (n * trades, sets), 1) == all_sets
    member = member.astype(F32).reshape(n, trades, sets)
    is_upper = (lax.broadcasted_iota(jnp.int32, (rows, sets), 0) // trades) % 2 == 1
    member_wide = jnp.concatenate([member, member], axis=1).reshape(rows, sets)
    member_low = jnp.where(is_upper, 0.0, member_wide).astype(BF16)
    member_high = jnp.where(is_upper, member_wide, 0.0).astype(BF16)
    net[:, :half] = dot(member_low, all_flows, TN).astype(BF16)
    net[:, half:] = dot(member_high, all_flows, TN)[:, : grid - half].astype(BF16)

    def value(i, carry):
        found = dot(features[i], net[...], NT)
        values[i] = found
        value_pair[core, pl.ds(i, 1), :] = jnp.sum(found, axis=0, keepdims=True)
        return carry

    lax.fori_loop(0, dates, value, 0)
    send_pair(value_pair.at[core], value_pair.at[core], 2).wait()
    send_sum(value_pair, value_sums, 3)
    wait_chips(value_sums, recv_sems, 3)
    offset = base_value[...] - jnp.sum(value_sums[...], axis=0) / paths_all
    weights = weight_rows[...]
    for i in range(dates):
        shifted = values[i] + offset[i : i + 1]
        slope = weights[i : i + 1] * jax.nn.sigmoid(SHARPNESS * shifted)
        total = jnp.sum(slope, axis=0, keepdims=True)
        slope_pair[core, i : i + 1, :] = total
        adjoint[i * paths : (i + 1) * paths, :] = (slope - total / paths).astype(BF16)
    slope_copy = send_pair(slope_pair.at[core], slope_pair.at[core], 4)
    weighted[...] = jnp.zeros_like(weighted)
    rate_acc[...] = jnp.zeros_like(rate_acc)
    loading_rows[...] = loading_rows[...] * jnp.exp(
        lax.broadcasted_iota(jnp.int32, (dates, grid), 0).astype(F32)
        * (-MEAN_REV * STEP_YEARS)
    )

    def backward(i, carry):
        adj = adjoint[pl.ds(pl.multiple_of(i * paths, paths), paths), :]
        date = pl.ds(i, 1)
        loading_row, horizon_row = loading_rows[date, :], horizon_rows[date, :]
        for at in pieces:
            product = dot(adj, net[:, at], NN) * exact[i, :, at]
            weighted[:, at] += loading_row[:, at] * product
            folded = jnp.sum(product.reshape(paths // 8, 8, at.stop - at.start), axis=0)
            rate_acc[:, at] += horizon_row[:, at] * folded
        return carry

    lax.fori_loop(0, dates // 4, backward, 0)
    slope_copy.wait()
    send_sum(slope_pair, slope_sums, 5)
    lax.fori_loop(dates // 4, dates, backward, 0)
    sums = dot(adjoint[...], features[...].reshape(dates * paths, grid), TN)

    wait_chips(slope_sums, recv_sems, 5)
    remainder = slope_pair[core] / paths - jnp.sum(slope_sums[...], axis=0) / paths_all
    common = dot(jnp.concatenate(split2(remainder), axis=0), net[...], NN)
    common = common[:dates] + common[dates:]
    rate = jnp.sum(rate_acc[...], axis=0, keepdims=True) + jnp.sum(
        horizon_rows[...] * common * exact_sums[...], axis=0, keepdims=True
    )
    rate = rate * (-1.0 / paths_all)
    lines = rate_sums.shape[1]
    for line in range(lines):
        first = 128 * line
        if first < grid:
            piece = rate[:, first : first + 128]
            rate_pair[core, line : line + 1, : piece.shape[1]] = piece
            if piece.shape[1] < 128:
                rate_pair[core, line : line + 1, piece.shape[1] :] = jnp.zeros(
                    (1, 128 - piece.shape[1]), F32
                )
        else:
            rate_pair[core, line : line + 1, :] = jnp.zeros((1, 128), F32)
    rate_copy = send_pair(rate_pair.at[core], rate_pair.at[core], 6)

    sums = sums + dot(remainder, feature_sums[...], TN, precision=lax.Precision.HIGHEST)
    sums = sums * (1.0 / paths_all)
    sums = jnp.concatenate([sums, jnp.zeros((sets, 2 * half - grid), F32)], axis=1)
    stacked = jnp.concatenate(split2(sums), axis=0)
    low_part = dot(all_flows, stacked[:, :half], NT)
    high_part = dot(all_flows, stacked[:, half:], NT)
    low_part = low_part[:, :sets] + low_part[:, sets:]
    high_part = high_part[:, :sets] + high_part[:, sets:]
    terms = jnp.where(is_upper, high_part, low_part) * member_wide
    terms = terms.reshape(2, chips, 2, trades, sets)
    alloc_sent[...] = terms[:, :, 0] + terms[:, :, 1]
    alloc_copy = send_pair(alloc_sent.at[1 - core], alloc_pair, 8)
    rate_copy.wait()
    send_sum(rate_pair, rate_sums, 7)

    loading_rows[...] = loading_rows[...] * common
    alloc_copy.wait()
    alloc_chip[...] = alloc_sent[core] + alloc_pair[...]
    alloc_sums[chip] = alloc_chip[chip]
    send_chips(lambda other: alloc_chip.at[other], alloc_sums, 9)

    load_high, load_low = split2(factor_load[...])
    load_both = jnp.concatenate([load_high, load_low], axis=0)
    local = jnp.zeros((factors, paths), F32)
    for at in pieces:
        held = weighted[:, at]
        for i in range(dates):
            held = held + loading_rows[i : i + 1, at] * exact[i, :, at]
        y_high, y_low = split2(held)
        both = dot(load_both[:, at], y_high, NT)
        local = local + (both[:factors] + both[factors:] + dot(load_high[:, at], y_low, NT))
    start_out[...] = DECAY**dates * later_adjoint[...] + DECAY * local

    wait_chips(rate_sums, recv_sems, 7)
    total = jnp.sum(rate_sums[...], axis=0)
    held = [None] * len(pieces)
    for line, rows_at in enumerate(pieces):
        count = rows_at.stop - rows_at.start
        column = row_to_column(total[line : line + 1, :count])
        for k, at in enumerate(pieces):
            product = spline[rows_at, at] * column
            product = jnp.sum(product.reshape(count // 8, 8, at.stop - at.start), axis=0)
            held[k] = product if line == 0 else held[k] + product
    for k, at in enumerate(pieces):
        knot_out[:, at] = jnp.sum(held[k], axis=0, keepdims=True)

    wait_chips(alloc_sums, recv_sems, 9)
    alloc_out[...] = column_to_row(
        jnp.sum(jnp.sum(alloc_sums[...], axis=0), axis=1, keepdims=True)
    )
    for buffer, which in ((value_sums, 3), (slope_sums, 5), (rate_sums, 7), (alloc_sums, 9)):
        wait_chips(buffer, send_sems, which)


def hand_on(knot_part, alloc_part, start_part, knot_out, alloc_out, start_out, sems):
    copies = []
    for source, target in (
        (start_part, start_out),
        (knot_part, knot_out),
        (alloc_part, alloc_out),
    ):
        copies.append(pltpu.make_async_copy(source, target, sems.at[len(copies)]))
        copies[-1].start()
    for copy in copies:
        copy.wait()


def per_device(
    normals,
    start_state,
    later_adjoint,
    vol,
    factor_load,
    knots,
    spline_jac,
    cashflows,
    trade_set,
    trade_end,
    set_cpty,
    default_prob,
    base_value,
):
    n = lax.axis_size("path")
    dates, factors, paths = normals.shape
    grid = knots.shape[0]
    trades = cashflows.shape[0]
    sets = base_value.shape[1]
    half = -(-(grid + 2) // 256) * 128
    lines = -(-grid // 1024) * 8
    vmem = pl.BlockSpec(memory_space=pltpu.VMEM)
    hbm = pl.BlockSpec(memory_space=pltpu.HBM)
    arguments = (
        trade_set.reshape(1, trades),
        trade_end.reshape(1, trades),
        spline_jac,
        knots.reshape(1, grid),
        factor_load,
        vol.reshape(1, dates),
        start_state,
        normals,
        set_cpty.reshape(1, sets),
        default_prob,
        base_value,
        later_adjoint,
    )
    out_shape = [
        jax.ShapeDtypeStruct((1, grid), F32),
        jax.ShapeDtypeStruct((1, trades), F32),
        jax.ShapeDtypeStruct((factors, paths), F32),
    ]
    parts = pl.pallas_call(
        functools.partial(kernel, n),
        out_shape=[pltpu.VMEM(each.shape, each.dtype) for each in out_shape],
        in_specs=[vmem] + [hbm] * len(arguments),
        out_specs=[vmem] * 3,
        scratch_shapes=[pltpu.VMEM(each.shape, each.dtype) for each in arguments]
        + [
            pltpu.VMEM((2, n // 2, 2 * trades, half), BF16),
            pltpu.VMEM((2, dates, sets), F32),
            pltpu.VMEM((n // 2, dates, sets), F32),
            pltpu.VMEM((2, dates, sets), F32),
            pltpu.VMEM((n // 2, dates, sets), F32),
            pltpu.VMEM((2, lines, 128), F32),
            pltpu.VMEM((n // 2, lines, 128), F32),
            pltpu.VMEM((2, n // 2, trades, sets), F32),
            pltpu.VMEM((n // 2, trades, sets), F32),
            pltpu.VMEM((n // 2, trades, sets), F32),
            pltpu.VMEM((n // 2, trades, sets), F32),
            pltpu.VMEM((sets, grid), BF16),
            pltpu.VMEM((dates, paths, grid), F32),
            pltpu.VMEM((dates, paths, grid), BF16),
            pltpu.VMEM((dates, paths, sets), F32),
            pltpu.VMEM((dates * paths, sets), BF16),
            pltpu.VMEM((paths, grid), F32),
            pltpu.VMEM((8, grid), F32),
            pltpu.VMEM((dates, grid), F32),
            pltpu.VMEM((dates, grid), F32),
            pltpu.VMEM((dates, grid), F32),
            pltpu.VMEM((dates, sets), F32),
            pltpu.VMEM((6 * factors, grid), BF16),
            pltpu.VMEM((dates, grid), F32),
            pltpu.VMEM((dates, grid), F32),
            pltpu.SemaphoreType.DMA((len(arguments),)),
            pltpu.SemaphoreType.DMA((10,)),
            pltpu.SemaphoreType.DMA((10,)),
        ],
        compiler_params=pltpu.CompilerParams(
            collective_id=0, has_side_effects=True, vmem_limit_bytes=58 * 1024 * 1024
        ),
    )(cashflows, *arguments)
    knot_grad, alloc, start_adjoint = pl.pallas_call(
        hand_on,
        out_shape=out_shape,
        in_specs=[vmem] * 3,
        out_specs=[hbm] * 3,
        scratch_shapes=[pltpu.SemaphoreType.DMA((3,))],
        compiler_params=pltpu.CompilerParams(vmem_limit_bytes=1024 * 1024),
    )(*parts)
    return knot_grad.reshape(grid), alloc.reshape(trades), start_adjoint


def solution(mesh):
    in_specs = (
        P(None, None, ("group", "path")),
        P(None, ("group", "path")),
        P(None, ("group", "path")),
        P(),
        P(),
        P(),
        P(),
        P(("group", "path"), None),
        P(("group", "path"), None),
        P(("group", "path")),
        P("group", None),
        P(),
        P(None, "group"),
    )
    out_specs = (P("group"), P(("group", "path")), P(None, ("group", "path")))
    return jax.shard_map(
        per_device, mesh=mesh, in_specs=in_specs, out_specs=out_specs, check_vma=False
    )
```

```python
import functools
import math

import jax
import jax.numpy as jnp
from jax import lax
from jax.experimental import pallas as pl
from jax.experimental.pallas import tpu as pltpu
from jax.sharding import PartitionSpec as P

MEAN_REV = 0.05
STEP_YEARS = 0.25
HORIZON_YEARS = 30.0
SHARPNESS = 4.0
LOSS_RATE = 0.6
DECAY = math.exp(-MEAN_REV * STEP_YEARS)
MESH = pl.DeviceIdType.MESH
F32 = jnp.float32
BF16 = jnp.bfloat16


def dot(a, b, dims, precision=None):
    return lax.dot_general(
        a, b, (dims, ((), ())), preferred_element_type=F32, precision=precision
    )


NN = ((1,), (0,))
NT = ((1,), (1,))
TN = ((0,), (0,))


def split3(x):
    high = x.astype(BF16)
    rest = x - high.astype(F32)
    mid = rest.astype(BF16)
    low = (rest - mid.astype(F32)).astype(BF16)
    return high, mid, low


def split2(x):
    high = x.astype(BF16)
    return high, (x - high.astype(F32)).astype(BF16)


def diagonal(rows):
    return lax.broadcasted_iota(jnp.int32, (rows, rows), 0) == lax.broadcasted_iota(
        jnp.int32, (rows, rows), 1
    )


def column_to_row(column):
    count = column.shape[0]
    pieces = []
    for first in range(0, count, 128):
        rows = min(128, count - first)
        piece = jnp.broadcast_to(column[first : first + rows], (rows, rows))
        pieces.append(jnp.sum(jnp.where(diagonal(rows), piece, 0.0), axis=0, keepdims=True))
    return jnp.concatenate(pieces, axis=1) if len(pieces) > 1 else pieces[0]


def row_to_column(row):
    count = row.shape[1]
    pieces = []
    for first in range(0, count, 128):
        rows = min(128, count - first)
        piece = jnp.broadcast_to(row[:, first : first + rows], (rows, rows))
        pieces.append(jnp.sum(jnp.where(diagonal(rows), piece, 0.0), axis=1, keepdims=True))
    return jnp.concatenate(pieces, axis=0) if len(pieces) > 1 else pieces[0]


def kernel(
    n,
    cashflows,
    trade_set_hbm,
    trade_end_hbm,
    spline_hbm,
    knots_hbm,
    factor_load_hbm,
    vol_hbm,
    start_state_hbm,
    normals_hbm,
    set_cpty_hbm,
    default_prob_hbm,
    base_value_hbm,
    later_adjoint_hbm,
    knot_out,
    alloc_out,
    start_out,
    trade_set,
    trade_end,
    spline,
    knots,
    factor_load,
    vol,
    start_state,
    normals,
    set_cpty,
    default_prob,
    base_value,
    later_adjoint,
    flows,
    value_pair,
    value_sums,
    slope_pair,
    slope_sums,
    rate_pair,
    rate_sums,
    alloc_sent,
    alloc_pair,
    alloc_chip,
    alloc_sums,
    net,
    exact,
    features,
    values,
    adjoint,
    weighted,
    rate_acc,
    loading_rows,
    discount_rows,
    horizon_rows,
    weight_rows,
    load_split,
    exact_sums,
    feature_sums,
    load_sems,
    send_sems,
    recv_sems,
):
    dates, factors, paths = normals.shape
    grid = knots.shape[1]
    trades = cashflows.shape[0]
    sets = base_value.shape[1]
    half = flows.shape[3]
    chips = n // 2
    short = chips <= 16
    paths_all = paths * n
    me = lax.axis_index("path")
    chip, core = me // 2, me % 2
    partner = me + 1 - 2 * core

    barrier = pltpu.get_barrier_semaphore()

    def greet(step, carry):
        pl.semaphore_signal(
            barrier, inc=1, device_id={"path": lax.rem(me + 2 * step, n)}, device_id_type=MESH
        )
        return carry

    lax.fori_loop(1, chips, greet, 0, unroll=short)
    pl.semaphore_signal(barrier, inc=1, device_id={"path": partner}, device_id_type=MESH)

    loads = []
    for source, target in (
        (trade_set_hbm, trade_set),
        (trade_end_hbm, trade_end),
        (spline_hbm, spline),
        (knots_hbm, knots),
        (factor_load_hbm, factor_load),
        (vol_hbm, vol),
        (start_state_hbm, start_state),
        (normals_hbm, normals),
        (set_cpty_hbm, set_cpty),
        (default_prob_hbm, default_prob),
        (base_value_hbm, base_value),
        (later_adjoint_hbm, later_adjoint),
    ):
        loads.append(pltpu.make_async_copy(source, target, load_sems.at[len(loads)]))
        loads[-1].start()

    loads[0].wait()
    loads[1].wait()
    set_id = row_to_column(trade_set[...].astype(F32)).astype(jnp.int32)
    end = row_to_column(trade_end[...].astype(F32)).astype(jnp.int32)
    live = jnp.where(
        lax.broadcasted_iota(jnp.int32, (trades, grid), 1) < end,
        cashflows[...].astype(F32),
        0.0,
    )
    upper = jnp.concatenate(
        [
            live[:, half:],
            jnp.zeros((trades, 2 * half - grid - 2), F32),
            (set_id // 128).astype(F32),
            (set_id % 128).astype(F32),
        ],
        axis=1,
    )
    flows[core, chip] = jnp.concatenate([live[:, :half], upper], axis=0).astype(BF16)

    pl.semaphore_wait(barrier, chips)

    def send_flows(step, carry):
        pltpu.make_async_remote_copy(
            src_ref=flows.at[core, chip],
            dst_ref=flows.at[core, chip],
            send_sem=send_sems.at[0],
            recv_sem=recv_sems.at[0],
            device_id={"path": lax.rem(me + 2 * step, n)},
            device_id_type=MESH,
        ).start()
        return carry

    lax.fori_loop(1, chips, send_flows, 0, unroll=short)

    def send_pair(buffer, target, which):
        copy = pltpu.make_async_remote_copy(
            src_ref=buffer,
            dst_ref=target,
            send_sem=send_sems.at[which],
            recv_sem=recv_sems.at[which],
            device_id={"path": partner},
            device_id_type=MESH,
        )
        copy.start()
        return copy

    def send_chips(source, buffer, which):
        def send(step, carry):
            other = lax.rem(chip + step, chips)
            pltpu.make_async_remote_copy(
                src_ref=source(other),
                dst_ref=buffer.at[chip],
                send_sem=send_sems.at[which],
                recv_sem=recv_sems.at[which],
                device_id={"path": 2 * other + core},
                device_id_type=MESH,
            ).start()
            return carry

        lax.fori_loop(1, chips, send, 0, unroll=short)

    def wait_chips(buffer, sems, which):
        others = buffer.at[pl.ds(0, chips - 1)]
        pltpu.make_async_copy(others, others, sems.at[which]).wait()

    def send_sum(pair, sums, which):
        sums[chip] = pair[0] + pair[1]
        send_chips(lambda other: sums.at[chip], sums, which)

    index = lax.broadcasted_iota(jnp.int32, (dates, grid), 1)
    date = lax.broadcasted_iota(jnp.int32, (dates, grid), 0)
    alive = 120 * (index + 1) > grid * (date + 1)
    maturity = HORIZON_YEARS * (index + 1).astype(F32) / grid
    fixing = STEP_YEARS * (date + 1).astype(F32)
    horizon = jnp.where(alive, maturity - fixing, 0.0)
    horizon_rows[...] = horizon
    loading_rows[...] = -((1.0 - jnp.exp(-MEAN_REV * horizon)) / MEAN_REV)
    for load in loads[2:]:
        load.wait()
    pieces = [slice(first, min(first + 128, grid)) for first in range(0, grid, 128)]
    zero_rows = []
    for rows_at in pieces:
        full = [at for at in pieces if at.stop - at.start == 128]
        held = spline[rows_at, full[0]] * knots[:, full[0]]
        for at in full[1:]:
            held = held + spline[rows_at, at] * knots[:, at]
        column = jnp.sum(held, axis=1, keepdims=True)
        if len(full) < len(pieces):
            at = pieces[-1]
            column = column + jnp.sum(spline[rows_at, at] * knots[:, at], axis=1, keepdims=True)
        zero_rows.append(column_to_row(column))
    zero_rate = jnp.concatenate(zero_rows, axis=1)
    discount_rows[...] = jnp.where(alive, jnp.exp(-zero_rate * horizon), 0.0)

    counter = (
        lax.broadcasted_iota(jnp.int32, (default_prob.shape[1], sets), 0) == set_cpty[...]
    ).astype(F32)
    weight_rows[...] = LOSS_RATE * dot(
        default_prob[...], counter, NN, precision=lax.Precision.HIGHEST
    )

    high, mid, low = split3(factor_load[...])
    load_split[...] = jnp.concatenate([high, high, mid, high, mid, low], axis=0)

    def forward(i, state):
        here = lax.broadcasted_iota(jnp.int32, (1, dates), 1) == i
        date_vol = jnp.sum(jnp.where(here, vol[...], 0.0), axis=1, keepdims=True)
        state = DECAY * state + date_vol * normals[i]
        s_high, s_mid, s_low = [part.astype(F32) for part in split3(state)]
        stacked = jnp.concatenate([s_high, s_mid, s_high, s_low, s_mid, s_high], axis=0)
        stacked = stacked.T.astype(BF16)
        date = pl.ds(i, 1)
        discount_row, loading_row = discount_rows[date, :], loading_rows[date, :]
        exact_row, feature_row = [], []
        for at in pieces:
            shift = dot(stacked, load_split[:, at], NN)
            feat = discount_row[:, at] * jnp.exp(loading_row[:, at] * shift)
            rounded = feat.astype(BF16)
            exact[i, :, at] = feat
            features[i, :, at] = rounded
            exact_row.append(jnp.sum(feat, axis=0, keepdims=True))
            feature_row.append(jnp.sum(rounded.astype(F32), axis=0, keepdims=True))
        exact_sums[date, :] = jnp.concatenate(exact_row, axis=1)
        feature_sums[date, :] = jnp.concatenate(feature_row, axis=1)
        return state

    early = dates - dates // 4
    state = lax.fori_loop(0, early, forward, start_state[...])
    part = flows.at[0, pl.ds(0, chips - 1)]
    pltpu.make_async_copy(part, part, recv_sems.at[0]).wait()
    share = pltpu.make_async_remote_copy(
        src_ref=flows.at[core],
        dst_ref=flows.at[core],
        send_sem=send_sems.at[1],
        recv_sem=recv_sems.at[1],
        device_id={"path": partner},
        device_id_type=MESH,
    )
    share.start()
    lax.fori_loop(early, dates, forward, state)
    pltpu.make_async_copy(part, part, send_sems.at[0]).wait()
    share.wait()

    rows = n * 2 * trades
    all_flows = flows[...].reshape(rows, half)
    tail = flows[:, :, :, half - 128 :].astype(F32).reshape(n, 2 * trades, 128)
    tail = tail[:, trades:].reshape(n * trades, 128)
    all_sets = (128.0 * tail[:, 126:127] + tail[:, 127:128]).astype(jnp.int32)
    member = lax.broadcasted_iota(jnp.int32, (n * trades, sets), 1) == all_sets
    member = member.astype(F32).reshape(n, trades, sets)
    is_upper = (lax.broadcasted_iota(jnp.int32, (rows, sets), 0) // trades) % 2 == 1
    member_wide = jnp.concatenate([member, member], axis=1).reshape(rows, sets)
    member_low = jnp.where(is_upper, 0.0, member_wide).astype(BF16)
    member_high = jnp.where(is_upper, member_wide, 0.0).astype(BF16)
    net[:, :half] = dot(member_low, all_flows, TN).astype(BF16)
    net[:, half:] = dot(member_high, all_flows, TN)[:, : grid - half].astype(BF16)

    def value(i, carry):
        found = dot(features[i], net[...], NT)
        values[i] = found
        value_pair[core, pl.ds(i, 1), :] = jnp.sum(found, axis=0, keepdims=True)
        return carry

    lax.fori_loop(0, dates, value, 0, unroll=True)
    value_copy = send_pair(value_pair.at[core], value_pair.at[core], 2)
    weighted[...] = jnp.zeros_like(weighted)
    rate_acc[...] = jnp.zeros_like(rate_acc)
    loading_rows[...] = loading_rows[...] * jnp.exp(
        lax.broadcasted_iota(jnp.int32, (dates, grid), 0).astype(F32)
        * (-MEAN_REV * STEP_YEARS)
    )
    value_copy.wait()
    send_sum(value_pair, value_sums, 3)
    wait_chips(value_sums, recv_sems, 3)
    offset = base_value[...] - jnp.sum(value_sums[...], axis=0) / paths_all
    weights = weight_rows[...]
    for i in range(dates):
        shifted = values[i] + offset[i : i + 1]
        slope = weights[i : i + 1] * jax.nn.sigmoid(SHARPNESS * shifted)
        total = jnp.sum(slope, axis=0, keepdims=True)
        slope_pair[core, i : i + 1, :] = total
        adjoint[i * paths : (i + 1) * paths, :] = (slope - total / paths).astype(BF16)
    slope_copy = send_pair(slope_pair.at[core], slope_pair.at[core], 4)

    def backward(i, carry):
        adj = adjoint[pl.ds(pl.multiple_of(i * paths, paths), paths), :]
        date = pl.ds(i, 1)
        loading_row, horizon_row = loading_rows[date, :], horizon_rows[date, :]
        for at in pieces:
            product = dot(adj, net[:, at], NN) * exact[i, :, at]
            weighted[:, at] += loading_row[:, at] * product
            folded = jnp.sum(product.reshape(paths // 8, 8, at.stop - at.start), axis=0)
            rate_acc[:, at] += horizon_row[:, at] * folded
        return carry

    lax.fori_loop(0, dates // 4, backward, 0, unroll=2)
    slope_copy.wait()
    send_sum(slope_pair, slope_sums, 5)
    lax.fori_loop(dates // 4, dates, backward, 0, unroll=2)
    sums = dot(adjoint[...], features[...].reshape(dates * paths, grid), TN)

    wait_chips(slope_sums, recv_sems, 5)
    remainder = slope_pair[core] / paths - jnp.sum(slope_sums[...], axis=0) / paths_all
    common = dot(jnp.concatenate(split2(remainder), axis=0), net[...], NN)
    common = common[:dates] + common[dates:]
    rate = jnp.sum(rate_acc[...], axis=0, keepdims=True) + jnp.sum(
        horizon_rows[...] * common * exact_sums[...], axis=0, keepdims=True
    )
    rate = rate * (-1.0 / paths_all)
    lines = rate_sums.shape[1]
    for line in range(lines):
        first = 128 * line
        if first < grid:
            piece = rate[:, first : first + 128]
            rate_pair[core, line : line + 1, : piece.shape[1]] = piece
            if piece.shape[1] < 128:
                rate_pair[core, line : line + 1, piece.shape[1] :] = jnp.zeros(
                    (1, 128 - piece.shape[1]), F32
                )
        else:
            rate_pair[core, line : line + 1, :] = jnp.zeros((1, 128), F32)
    rate_copy = send_pair(rate_pair.at[core], rate_pair.at[core], 6)

    sums = sums + dot(remainder, feature_sums[...], TN, precision=lax.Precision.HIGHEST)
    sums = sums * (1.0 / paths_all)
    sums = jnp.concatenate([sums, jnp.zeros((sets, 2 * half - grid), F32)], axis=1)
    stacked = jnp.concatenate(split2(sums), axis=0)
    low_part = dot(all_flows, stacked[:, :half], NT)
    high_part = dot(all_flows, stacked[:, half:], NT)
    low_part = low_part[:, :sets] + low_part[:, sets:]
    high_part = high_part[:, :sets] + high_part[:, sets:]
    terms = jnp.where(is_upper, high_part, low_part) * member_wide
    terms = terms.reshape(2, chips, 2, trades, sets)
    alloc_sent[...] = terms[:, :, 0] + terms[:, :, 1]
    alloc_copy = send_pair(alloc_sent.at[1 - core], alloc_pair, 8)
    rate_copy.wait()
    send_sum(rate_pair, rate_sums, 7)

    loading_rows[...] = loading_rows[...] * common
    load_high, load_low = split2(factor_load[...])
    load_both = jnp.concatenate([load_high, load_low], axis=0)

    def last_product(some):
        local = jnp.zeros((factors, paths), F32)
        for at in some:
            held = weighted[:, at]
            for i in range(dates):
                held = held + loading_rows[i : i + 1, at] * exact[i, :, at]
            y_high, y_low = split2(held)
            both = dot(load_both[:, at], y_high, NT)
            local = local + (both[:factors] + both[factors:] + dot(load_high[:, at], y_low, NT))
        return local

    middle = len(pieces) // 2
    local = last_product(pieces[:middle])
    alloc_copy.wait()
    alloc_chip[...] = alloc_sent[core] + alloc_pair[...]
    alloc_sums[chip] = alloc_chip[chip]
    send_chips(lambda other: alloc_chip.at[other], alloc_sums, 9)
    local = local + last_product(pieces[middle:])
    start_out[...] = DECAY**dates * later_adjoint[...] + DECAY * local

    wait_chips(rate_sums, recv_sems, 7)
    total = jnp.sum(rate_sums[...], axis=0)
    held = [None] * len(pieces)
    for line, rows_at in enumerate(pieces):
        count = rows_at.stop - rows_at.start
        column = row_to_column(total[line : line + 1, :count])
        for k, at in enumerate(pieces):
            product = spline[rows_at, at] * column
            product = jnp.sum(product.reshape(count // 8, 8, at.stop - at.start), axis=0)
            held[k] = product if line == 0 else held[k] + product
    for k, at in enumerate(pieces):
        knot_out[:, at] = jnp.sum(held[k], axis=0, keepdims=True)

    wait_chips(alloc_sums, recv_sems, 9)
    alloc_out[...] = column_to_row(
        jnp.sum(jnp.sum(alloc_sums[...], axis=0), axis=1, keepdims=True)
    )
    for buffer, which in ((value_sums, 3), (slope_sums, 5), (rate_sums, 7), (alloc_sums, 9)):
        wait_chips(buffer, send_sems, which)


def hand_on(knot_part, alloc_part, start_part, knot_out, alloc_out, start_out, sems):
    copies = []
    for source, target in (
        (start_part, start_out),
        (knot_part, knot_out),
        (alloc_part, alloc_out),
    ):
        copies.append(pltpu.make_async_copy(source, target, sems.at[len(copies)]))
        copies[-1].start()
    for copy in copies:
        copy.wait()


def per_device(
    normals,
    start_state,
    later_adjoint,
    vol,
    factor_load,
    knots,
    spline_jac,
    cashflows,
    trade_set,
    trade_end,
    set_cpty,
    default_prob,
    base_value,
):
    n = lax.axis_size("path")
    dates, factors, paths = normals.shape
    grid = knots.shape[0]
    trades = cashflows.shape[0]
    sets = base_value.shape[1]
    half = -(-(grid + 2) // 256) * 128
    lines = -(-grid // 1024) * 8
    vmem = pl.BlockSpec(memory_space=pltpu.VMEM)
    hbm = pl.BlockSpec(memory_space=pltpu.HBM)
    arguments = (
        trade_set.reshape(1, trades),
        trade_end.reshape(1, trades),
        spline_jac,
        knots.reshape(1, grid),
        factor_load,
        vol.reshape(1, dates),
        start_state,
        normals,
        set_cpty.reshape(1, sets),
        default_prob,
        base_value,
        later_adjoint,
    )
    out_shape = [
        jax.ShapeDtypeStruct((1, grid), F32),
        jax.ShapeDtypeStruct((1, trades), F32),
        jax.ShapeDtypeStruct((factors, paths), F32),
    ]
    parts = pl.pallas_call(
        functools.partial(kernel, n),
        out_shape=[pltpu.VMEM(each.shape, each.dtype) for each in out_shape],
        in_specs=[vmem] + [hbm] * len(arguments),
        out_specs=[vmem] * 3,
        scratch_shapes=[pltpu.VMEM(each.shape, each.dtype) for each in arguments]
        + [
            pltpu.VMEM((2, n // 2, 2 * trades, half), BF16),
            pltpu.VMEM((2, dates, sets), F32),
            pltpu.VMEM((n // 2, dates, sets), F32),
            pltpu.VMEM((2, dates, sets), F32),
            pltpu.VMEM((n // 2, dates, sets), F32),
            pltpu.VMEM((2, lines, 128), F32),
            pltpu.VMEM((n // 2, lines, 128), F32),
            pltpu.VMEM((2, n // 2, trades, sets), F32),
            pltpu.VMEM((n // 2, trades, sets), F32),
            pltpu.VMEM((n // 2, trades, sets), F32),
            pltpu.VMEM((n // 2, trades, sets), F32),
            pltpu.VMEM((sets, grid), BF16),
            pltpu.VMEM((dates, paths, grid), F32),
            pltpu.VMEM((dates, paths, grid), BF16),
            pltpu.VMEM((dates, paths, sets), F32),
            pltpu.VMEM((dates * paths, sets), BF16),
            pltpu.VMEM((paths, grid), F32),
            pltpu.VMEM((8, grid), F32),
            pltpu.VMEM((dates, grid), F32),
            pltpu.VMEM((dates, grid), F32),
            pltpu.VMEM((dates, grid), F32),
            pltpu.VMEM((dates, sets), F32),
            pltpu.VMEM((6 * factors, grid), BF16),
            pltpu.VMEM((dates, grid), F32),
            pltpu.VMEM((dates, grid), F32),
            pltpu.SemaphoreType.DMA((len(arguments),)),
            pltpu.SemaphoreType.DMA((10,)),
            pltpu.SemaphoreType.DMA((10,)),
        ],
        compiler_params=pltpu.CompilerParams(
            collective_id=0, has_side_effects=True, vmem_limit_bytes=58 * 1024 * 1024
        ),
    )(cashflows, *arguments)
    knot_grad, alloc, start_adjoint = pl.pallas_call(
        hand_on,
        out_shape=out_shape,
        in_specs=[vmem] * 3,
        out_specs=[hbm] * 3,
        scratch_shapes=[pltpu.SemaphoreType.DMA((3,))],
        compiler_params=pltpu.CompilerParams(vmem_limit_bytes=1024 * 1024),
    )(*parts)
    return knot_grad.reshape(grid), alloc.reshape(trades), start_adjoint


def solution(mesh):
    in_specs = (
        P(None, None, ("group", "path")),
        P(None, ("group", "path")),
        P(None, ("group", "path")),
        P(),
        P(),
        P(),
        P(),
        P(("group", "path"), None),
        P(("group", "path"), None),
        P(("group", "path")),
        P("group", None),
        P(),
        P(None, "group"),
    )
    out_specs = (P("group"), P(("group", "path")), P(None, ("group", "path")))
    return jax.shard_map(
        per_device, mesh=mesh, in_specs=in_specs, out_specs=out_specs, check_vma=False
    )
```
